256 devices in a mesh: dp: 32 (over y, z_lo, core), tensor: 8 (over z_hi, x).
Axes of the slice: x: 4, y: 4, z: 8 (z_hi: 2, z_lo: 4; z = z_hi * 4 + z_lo), core: 2. Of those that a mesh axis runs over, the one named last changes fastest.
Arguments:
- stream_in: bfloat16 [4096, 4096], P(('dp', 'tensor')), may hold values from -6 to 6
- pending: bfloat16 [8, 4096, 4096], P('tensor', 'dp'), may hold values from -6 to 6
- gain: float32 [4096], replicated, may hold values from 0.5 to 1.5
- q_weight: bfloat16 [4096, 4096], P('dp', 'tensor'), may hold values from -1 to 1
- k_weight: bfloat16 [4096, 512], P('dp'), may hold values from -4 to 4
- v_weight: bfloat16 [4096, 512], P('dp'), may hold values from -0.09375 to 0.09375
- out_weight: bfloat16 [4096, 4096], P('dp', 'tensor'), may hold values from -0.09375 to 0.09375
- grad_out: bfloat16 [4096, 4096], P(('dp', 'tensor')), may hold values from -6 to 6
- doc_ids: int32 [4096], replicated, may hold values from 0 to 5, never falling along the last dimension, each value on 1 to 3072 neighbouring positions
Outputs:
- hidden_out: bfloat16 [4096, 4096], P(('dp', 'tensor'))
- grad_stream: bfloat16 [4096, 4096], P(('dp', 'tensor'))
- grad_gain: float32 [4096], replicated
- grad_q: float32 [4096, 4096], P('dp', 'tensor')
- grad_k: float32 [4096, 512], P('dp')
- grad_v: float32 [4096, 512], P('dp')
- grad_o: float32 [4096, 4096], P('dp', 'tensor')
The draws below stay inside these ranges and needn't reach their ends.
Inputs may be any that keep to these rules, and one draw needn't show every extreme that they name: `doc_ids`: never falls along the positions; the longest document has exactly 3072 positions.
All inputs are finite; a program needn't handle non-finite values.
Results may differ from the reference program's by a relative error of at most 0.035.
The reference program's roundings to bfloat16 on the way count: a program that leaves them out, or rounds other values in their place, can miss the bound.
Values may be sent and summed in bfloat16 or wider, within the bound.
No kernel may reach another device: no remote copies, remote signals or barrier semaphores. Data moves between devices by JAX's collectives and lax.ppermute only.
A program may use at most 128 MiB of HBM per device.

```python
import math
import jax
import jax.numpy as jnp
import numpy as np
from jax import lax

D = 4096
HEADS = 32
KV_HEADS = 4
HEAD_DIM = 128
DOCS = 6
TOK_DEV = 128
SEQ_LEN = 4096
TOKENS = 4096
N_DP = 32
N_TENSOR = 8


def shared_base(key):
    base = jax.random.normal(key, (D, HEADS * HEAD_DIM), jnp.float32)
    return jnp.clip(base, -5.0, 5.0) * (1.0 / math.sqrt(D))


def draw_q_weight(key, part):
    base = shared_base(key)
    return base.astype(jnp.bfloat16)


def draw_k_weight(key, part):
    key = jax.random.fold_in(key, 5)
    noise = jnp.clip(jax.random.normal(key, (D, KV_HEADS * HEAD_DIM), jnp.float32), -5.0, 5.0) * (1.0 / math.sqrt(D))
    return noise.astype(jnp.bfloat16)


def levels(stream_key, extent, split, smallest, high):
    factor_of, own = 1.0, jax.random.fold_in(stream_key, 6)
    for axis_at, shards_of in split:
        steps = jnp.exp(jax.random.uniform(jax.random.fold_in(own, axis_at), (shards_of,), jnp.float32, smallest / len(split), high / len(split)))
        factor_of = factor_of * jnp.repeat(steps, extent[axis_at] // shards_of).reshape([-1 if axis == axis_at else 1 for axis in range(len(extent))])
    return factor_of


def profile(number_of, total, bound, slope):
    portions = [(1 << 20) // math.isqrt(grade ** slope) + 1 for grade in range(2, number_of + 1)]
    surplus, holding = total - bound - (number_of - 1), [1] * (number_of - 1)
    while surplus > 0:
        free = [i for i in range(number_of - 1) if holding[i] < bound]
        whole, left = sum([portions[i] for i in free]), surplus
        for i in free:
            extra = min(bound - holding[i], max(1, left * portions[i] // whole), surplus)
            holding[i] = holding[i] + extra
            surplus = surplus - extra
    return np.array([bound] + holding)


def uneven(stream_key, count, total, limit, lean):
    if count == 2:
        one = jax.random.randint(stream_key, (), max(1, total - limit), min(limit, total - 1) + 1)
        return jnp.stack([one, total - one])
    sizes = jnp.asarray(profile(count, total, limit, lean), jnp.int32)
    twos = (count - 1) // 2
    source_of, receiver = sizes[1:1 + 2 * twos:2], sizes[2:2 + 2 * twos:2]
    margin = jnp.minimum(source_of - 1, limit - receiver)
    shifted = jax.random.randint(jax.random.fold_in(stream_key, 1), (twos,), 0, 1 << 20) % (margin + 1)
    sizes = sizes.at[1:1 + 2 * twos:2].set(source_of - shifted).at[2:2 + 2 * twos:2].set(receiver + shifted)
    return sizes[jax.random.permutation(jax.random.fold_in(stream_key, 2), count)]


def bell_draw(stream_key, shape, spread, reach, split=(), held_as=jnp.bfloat16):
    result = jax.random.normal(stream_key, shape, jnp.float32) * spread
    if len(split) > 0:
        result = levels(stream_key, shape, split, -0.22, 0.18) * result
    return jnp.clip(result, min=-reach, max=reach).astype(held_as)


def setup_inputs(seed: int = 0) -> dict:
    streams_of = jax.random.split(jax.random.key(seed), 10)
    stream_in = bell_draw(streams_of[0], (TOKENS, D), 1.0, 6.0, ((0, 256),))
    pending = bell_draw(streams_of[1], (N_TENSOR, TOKENS, D), 0.5, 6.0, ((0, 8), (1, 32)))
    gain = jnp.clip(1.0 + 0.1 * jax.random.normal(streams_of[2], (D,), jnp.float32), 0.5, 1.5)
    q_weight = draw_q_weight(jax.random.fold_in(streams_of[9], 71), 0)
    k_weight = draw_k_weight(jax.random.fold_in(streams_of[9], 71), 0)
    v_weight = bell_draw(streams_of[5], (D, KV_HEADS * HEAD_DIM), D ** -0.5, 0.09375, ((0, 32),))
    out_weight = bell_draw(streams_of[6], (D, HEADS * HEAD_DIM), (HEADS * HEAD_DIM) ** -0.5, 0.09375, ((0, 32), (1, 8)))
    grad_out = bell_draw(streams_of[7], (TOKENS, D), 1.0, 6.0, ((0, 256),))
    doc_ids = jnp.searchsorted(jnp.cumsum(uneven(streams_of[8], DOCS, TOKENS, 3 * SEQ_LEN // 4, 2)), jnp.arange(TOKENS), side="right").astype(jnp.int32)
    return dict(stream_in=stream_in, pending=pending, gain=gain, q_weight=q_weight, k_weight=k_weight, v_weight=v_weight, out_weight=out_weight, grad_out=grad_out, doc_ids=doc_ids)


eps = 1e-05
rope_base = 500000.0

def rotate(field, positions, sign):
    half = field.shape[-1] // 2
    frequency = rope_base ** (-2.0 * jnp.arange(half).astype(field.dtype) / field.shape[-1])
    angles = positions.astype(field.dtype)[:, None] * frequency[None, :]
    cosine = jnp.cos(angles)[:, None, :]
    sine = sign * jnp.sin(angles)[:, None, :]
    first = field[..., :half]
    second = field[..., half:]
    return jnp.concatenate([first * cosine - second * sine, second * cosine + first * sine], axis=-1)

def attend_probs(query_b, keys, allowed, scale):
    scores = jnp.einsum('qghd,kgd->ghqk', query_b.astype(jnp.float32), keys.astype(jnp.float32)) * scale
    scores = jnp.where(allowed[None, None], scores, -1e+30)
    peak = lax.optimization_barrier(jnp.max(scores, axis=-1, keepdims=True))
    exp_terms = jnp.exp(scores - peak)
    return exp_terms / lax.optimization_barrier(jnp.sum(exp_terms, axis=-1, keepdims=True))

def round_up(value):
    return lax.optimization_barrier(value.astype(jnp.bfloat16)).astype(jnp.float32)

def block_sum(left, right):

    def step(carry, item):
        return (carry + round_up(jnp.dot(item[0].T, item[1], preferred_element_type=jnp.float32)), None)
    start = jnp.zeros((left.shape[2], right.shape[2]), jnp.float32)
    return lax.scan(step, start, (left, right))[0]

def reference(stream_in, pending, gain, q_weight, k_weight, v_weight, out_weight, grad_out, doc_ids):
    f_wide = jnp.float32
    f_low = jnp.bfloat16
    q_local = HEADS // N_TENSOR
    kv_local = max(KV_HEADS // N_TENSOR, 1)
    per_group = q_local // kv_local
    group = HEADS // KV_HEADS
    scale = HEAD_DIM ** (-0.5)
    q_width = q_local * HEAD_DIM
    k_width = kv_local * HEAD_DIM
    stream_f = stream_in.astype(f_wide)
    inv_rms = lax.rsqrt(lax.optimization_barrier(jnp.mean(stream_f * stream_f, axis=-1, keepdims=True)) + eps)
    unit_rows = stream_f * inv_rms
    normed = (unit_rows * gain).astype(f_low)
    positions = jnp.arange(TOKENS).astype(jnp.int32)
    places = positions % SEQ_LEN
    seq_of = positions // SEQ_LEN
    normed_blocks = normed.reshape(N_DP, TOK_DEV, D)
    cotan_blocks = grad_out.reshape(N_DP, TOK_DEV, D)
    place_blocks = positions.reshape(N_DP, TOK_DEV)
    doc_blocks = doc_ids.reshape(N_DP, TOK_DEV)
    pending_sum = jnp.zeros((TOKENS, D), f_wide)
    attn_sum = jnp.zeros((TOKENS, D), f_wide)
    grad_normed = jnp.zeros((TOKENS, D), f_wide)
    grad_k = jnp.zeros((D, KV_HEADS * HEAD_DIM), f_wide)
    grad_v = jnp.zeros((D, KV_HEADS * HEAD_DIM), f_wide)
    grad_q_parts = []
    grad_o_parts = []

    def mask_for(place_b, doc_b):
        same_seq = seq_of[None, :] == (place_b // SEQ_LEN)[:, None]
        return same_seq & (positions[None, :] <= place_b[:, None]) & (doc_ids[None, :] == doc_b[:, None])
    for tensor_idx in range(N_TENSOR):
        first = tensor_idx * q_width
        kv_first = tensor_idx * q_local // group * HEAD_DIM
        weights = jnp.concatenate([q_weight[:, first:first + q_width], k_weight[:, kv_first:kv_first + k_width], v_weight[:, kv_first:kv_first + k_width]], axis=1)
        projected = jnp.dot(normed, weights, preferred_element_type=f_wide)
        query = rotate(projected[:, :q_width].reshape(TOKENS, q_local, HEAD_DIM), places, 1.0).astype(f_low)
        query = query.reshape(TOKENS, kv_local, per_group, HEAD_DIM)
        keys = rotate(projected[:, q_width:q_width + k_width].reshape(TOKENS, kv_local, HEAD_DIM), places, 1.0).astype(f_low)
        values = projected[:, q_width + k_width:].reshape(TOKENS, kv_local, HEAD_DIM).astype(f_low)
        query_blocks = query.reshape(N_DP, TOK_DEV, kv_local, per_group, HEAD_DIM)

        def forward_block(item):
            query_b, place_b, doc_b = item
            prob_rows = attend_probs(query_b, keys, mask_for(place_b, doc_b), scale)
            attended = jnp.einsum('ghqk,kgd->qghd', round_up(prob_rows), values.astype(f_wide))
            return attended.astype(f_low)
        attended = lax.map(forward_block, (query_blocks, place_blocks, doc_blocks)).reshape(TOKENS, q_width)
        w_out = out_weight[:, first:first + q_width]
        attn_sum = attn_sum + round_up(jnp.dot(attended, w_out.T, preferred_element_type=f_wide))
        pending_sum = pending_sum + pending[tensor_idx].astype(f_wide)
        grad_o_parts.append(block_sum(cotan_blocks, attended.reshape(N_DP, TOK_DEV, q_width)))
        grad_heads = jnp.dot(grad_out, w_out, preferred_element_type=f_wide).astype(f_low)
        heads_blocks = grad_heads.reshape(N_DP, TOK_DEV, kv_local, per_group, HEAD_DIM)
        attn_blocks = attended.reshape(N_DP, TOK_DEV, kv_local, per_group, HEAD_DIM)

        def backward_block(item):
            query_b, place_b, doc_b, heads_b, attn_b = item
            prob_rows = attend_probs(query_b, keys, mask_for(place_b, doc_b), scale)
            delta = lax.optimization_barrier(jnp.sum(heads_b.astype(f_wide) * attn_b.astype(f_wide), axis=-1))
            delta = jnp.transpose(delta, (1, 2, 0))[..., None]
            grad_prob = jnp.einsum('qghd,kgd->ghqk', heads_b.astype(f_wide), values.astype(f_wide))
            grad_score = round_up(prob_rows * (grad_prob - delta))
            grad_query = jnp.einsum('ghqk,kgd->qghd', grad_score, keys.astype(f_wide)) * scale
            grad_key = (jnp.einsum('ghqk,qghd->kgd', grad_score, query_b.astype(f_wide)) * scale).astype(f_low)
            grad_value = jnp.einsum('ghqk,qghd->kgd', round_up(prob_rows), heads_b.astype(f_wide)).astype(f_low)
            return (grad_query, grad_key, grad_value)
        grad_query, key_terms, value_terms = lax.map(backward_block, (query_blocks, place_blocks, doc_blocks, heads_blocks, attn_blocks))
        grad_query = rotate(grad_query.reshape(TOKENS, q_local, HEAD_DIM), places, -1.0).astype(f_low).reshape(TOKENS, q_width)
        grad_key = rotate(lax.optimization_barrier(jnp.sum(key_terms.astype(f_wide), axis=0)), places, -1.0).astype(f_low).reshape(TOKENS, k_width)
        grad_value = lax.optimization_barrier(jnp.sum(value_terms.astype(f_wide), axis=0)).astype(f_low).reshape(TOKENS, k_width)
        grad_proj = jnp.concatenate([grad_query, grad_key, grad_value], axis=1)
        grad_w = block_sum(normed_blocks, grad_proj.reshape(N_DP, TOK_DEV, q_width + 2 * k_width))
        grad_q_parts.append(grad_w[:, :q_width])
        grad_k = grad_k.at[:, kv_first:kv_first + k_width].add(grad_w[:, q_width:q_width + k_width])
        grad_v = grad_v.at[:, kv_first:kv_first + k_width].add(grad_w[:, q_width + k_width:])
        grad_normed = grad_normed + round_up(jnp.dot(grad_proj, weights.T, preferred_element_type=f_wide))
    hidden_out = (stream_f + pending_sum + attn_sum).astype(f_low)
    grad_gain = lax.optimization_barrier(jnp.sum(grad_normed * unit_rows, axis=0))
    scaled_grad = grad_normed * gain
    grad_stream = (inv_rms * (scaled_grad - unit_rows * lax.optimization_barrier(jnp.mean(scaled_grad * unit_rows, axis=-1, keepdims=True))) + grad_out.astype(f_wide)).astype(f_low)
    return (hidden_out, grad_stream, grad_gain, jnp.concatenate(grad_q_parts, axis=1), grad_k, grad_v, jnp.concatenate(grad_o_parts, axis=1))
```

```python
import jax
import jax.numpy as jnp
from jax import lax
from jax.sharding import Mesh
from jax.sharding import PartitionSpec as P

HEADS = 32
KV_HEADS = 4
HEAD_DIM = 128
HALF_DIM = HEAD_DIM // 2

eps = 1e-05
rope_base = 500000.0

SIZES = {"y": 4, "z": 4, "c": 2, "h": 2, "x": 4}
DP = ("y", "z", "c")
TENSOR = ("h", "x")
wide = jnp.float32
low = jnp.bfloat16


def dot(a, b, dims):
    return lax.dot_general(a, b, (dims, ((), ())), preferred_element_type=wide)


def swap(a, axis):
    return lax.ppermute(a, axis, [(0, 1), (1, 0)])


def spread(a, axis):
    size = SIZES[axis]
    return lax.all_to_all(
        jnp.broadcast_to(a[None], (size,) + a.shape), axis, 0, 0, tiled=True
    )


def spread_yz(a):
    rows, cols = a.shape
    a = spread(a, "z").reshape(SIZES["z"] * rows, cols)
    return spread(a, "y").reshape(SIZES["y"] * SIZES["z"] * rows, cols)


def collect(a, axis):
    return jnp.sum(lax.all_to_all(a, axis, 0, 0, tiled=True).astype(wide), axis=0)


def collect_yz(a):
    rows, cols = a.shape
    a = collect(a.reshape(SIZES["y"], rows // SIZES["y"], cols), "y").astype(low)
    return collect(a.reshape(SIZES["z"], a.shape[0] // SIZES["z"], cols), "z")


def on_device(
    stream_in, pending, gain, q_weight, k_weight, v_weight, out_weight, grad_out, doc_ids
):
    y, z, c, h, x = (lax.axis_index(a) for a in ("y", "z", "c", "h", "x"))
    tens_index = h * SIZES["x"] + x
    rows_own, width = stream_in.shape
    tok = pending.shape[1]
    outer = SIZES["y"] * SIZES["z"]
    half_width = width // 2
    q_width = q_weight.shape[1]
    heads = q_width // HEAD_DIM
    seq_len = doc_ids.shape[0]
    scale = HEAD_DIM ** (-0.5)

    def columns(a, which):
        split = a.reshape(a.shape[0], outer, 2, width // outer // 2)
        return lax.dynamic_index_in_dim(split, which, 2, keepdims=False).reshape(
            a.shape[0], half_width
        )

    def spread_rows(a):
        pair = jnp.stack([columns(a, c), swap(columns(a, 1 - c), "c")])
        both = jnp.stack([pair, swap(pair, "h")])
        return spread(both, "x").reshape(2 * tok, half_width)

    def join(own, sibling):
        cols = own.shape[1]
        parts = [a.reshape(tok // rows_own, rows_own, cols) for a in (own, sibling)]
        return jnp.stack(parts, axis=1).reshape(2 * tok, cols)

    def join_cores(own):
        return join(own, swap(own, "c"))

    def sum_cores(a):
        split = a.reshape(tok // rows_own, 2, rows_own, a.shape[1])
        own, sibling = (split[:, i].reshape(tok, a.shape[1]) for i in range(2))
        return own + swap(sibling, "c")

    def collect_rows(a):
        a = collect(a.reshape(SIZES["x"], 2 * tok // SIZES["x"], half_width), "x")
        a = a.reshape(2, 2, rows_own, half_width)
        a = a[0] + swap(a[1].astype(low), "h").astype(wide)
        own, other = a[0], swap(a[1], "c")
        own, other = (b.reshape(rows_own, outer, 1, width // outer // 2) for b in (own, other))
        first, second = jnp.where(c == 0, own, other), jnp.where(c == 0, other, own)
        return jnp.concatenate([first, second], axis=2).reshape(rows_own, width)

    kv_first = tens_index * heads // (HEADS // KV_HEADS) * HEAD_DIM
    kv_weight = jnp.concatenate(
        [lax.dynamic_slice_in_dim(w, kv_first, HEAD_DIM, 1) for w in (k_weight, v_weight)], axis=1
    )
    wkv = spread_yz(kv_weight)
    wq = spread_yz(q_weight)
    wo = spread_yz(out_weight)

    stream_f = stream_in.astype(wide)
    inv_rms = lax.rsqrt(jnp.mean(stream_f * stream_f, axis=-1, keepdims=True) + eps)
    unit_rows = stream_f * inv_rms
    normed = spread_rows((unit_rows * gain).astype(low))
    grads = spread_rows(grad_out)

    rel_h = lax.broadcasted_iota(jnp.int32, (SIZES["x"], 2, rows_own), 1)
    at_x = lax.broadcasted_iota(jnp.int32, (SIZES["x"], 2, rows_own), 0)
    at_r = lax.broadcasted_iota(jnp.int32, (SIZES["x"], 2, rows_own), 2)
    local = (((h ^ rel_h) * SIZES["x"] + at_x) * rows_own + at_r).reshape(tok)
    block_first = ((y * SIZES["z"] + z) * 2 + c) * tok
    places = block_first + local
    rel_c = jnp.arange(2, dtype=jnp.int32)[:, None, None]
    at_yz = jnp.arange(outer, dtype=jnp.int32)[None, :, None]
    key_place = ((at_yz * 2 + (c ^ rel_c)) * tok + local[None, None, :]).reshape(seq_len)
    doc_block = lax.dynamic_slice_in_dim(doc_ids, block_first, tok)
    doc_block = doc_block.reshape(2, SIZES["x"], rows_own)
    doc_block = jnp.where(h == 0, doc_block, doc_block[::-1])
    doc_query = jnp.transpose(doc_block, (1, 0, 2)).reshape(tok)
    first_place = jnp.sum((doc_ids[None, :] < doc_query[:, None]).astype(jnp.int32), axis=1)
    allowed = (key_place[None, :] <= places[:, None]) & (key_place[None, :] >= first_place[:, None])

    frequency = rope_base ** (-2.0 * jnp.arange(HALF_DIM).astype(wide) / HEAD_DIM)
    angles = places.astype(wide)[:, None] * frequency[None, :]
    cosine, sine = jnp.cos(angles)[:, None, :], jnp.sin(angles)[:, None, :]

    def rotate(field, sign):
        first, second = field[..., :HALF_DIM], field[..., HALF_DIM:]
        return jnp.concatenate(
            [first * cosine - sign * second * sine, second * cosine + sign * first * sine], axis=-1
        )

    kv_proj = sum_cores(dot(normed, wkv, ((1,), (0,))))
    keys_own = rotate(kv_proj[:, :HEAD_DIM].reshape(tok, 1, HEAD_DIM), 1.0).reshape(tok, HEAD_DIM)
    kv_own = jnp.concatenate([keys_own, kv_proj[:, HEAD_DIM:]], axis=1).astype(low)
    kv_near = spread_yz(kv_own)
    kv_all = jnp.concatenate([kv_near, swap(kv_near, "c")], axis=0)
    keys, values = kv_all[:, :HEAD_DIM], kv_all[:, HEAD_DIM:]

    q_proj = sum_cores(dot(normed, wq, ((1,), (0,))))
    query = rotate(q_proj.reshape(tok, heads, HEAD_DIM), 1.0).astype(low)
    query = jnp.transpose(query, (1, 0, 2)).reshape(heads * tok, HEAD_DIM)
    grad_heads = sum_cores(dot(grads, wo, ((1,), (0,)))).astype(low)
    grad_heads = jnp.transpose(grad_heads.reshape(tok, heads, HEAD_DIM), (1, 0, 2))
    grad_heads = grad_heads.reshape(heads * tok, HEAD_DIM)

    scores = dot(query, keys, ((1,), (1,))).reshape(heads, tok, seq_len) * scale
    scores = jnp.where(allowed[None], scores, -1e30)
    peak = jnp.max(scores, axis=-1, keepdims=True)
    exp_terms = jnp.exp(scores - peak)
    prob = (exp_terms / jnp.sum(exp_terms, axis=-1, keepdims=True)).reshape(heads * tok, seq_len)
    prob_low = prob.astype(low)
    attended_h = dot(prob_low, values, ((1,), (0,))).astype(low)
    attended = jnp.transpose(attended_h.reshape(heads, tok, HEAD_DIM), (1, 0, 2))
    attended = join_cores(attended.reshape(tok, q_width))

    grad_o = collect_yz(dot(grads, attended, ((0,), (0,))).astype(low))

    delta = jnp.sum(grad_heads.astype(wide) * attended_h.astype(wide), axis=-1, keepdims=True)
    grad_prob = dot(grad_heads, values, ((1,), (1,)))
    grad_score = (prob * (grad_prob - delta)).astype(low)
    key_piece = dot(grad_score, query, ((0,), (0,))) * scale
    value_piece = dot(prob_low, grad_heads, ((0,), (0,)))
    kv_piece = jnp.concatenate([key_piece, value_piece], axis=1).astype(low)
    kv_sum = kv_piece[: seq_len // 2].astype(wide) + swap(kv_piece[seq_len // 2 :], "c").astype(wide)
    kv_grad = collect_yz(kv_sum.astype(low))

    grad_query = (dot(grad_score, keys, ((1,), (0,))) * scale).reshape(heads, tok, HEAD_DIM)
    grad_query = rotate(jnp.transpose(grad_query, (1, 0, 2)), -1.0).astype(low)
    grad_query = join_cores(grad_query.reshape(tok, q_width))
    grad_q = collect_yz(dot(normed, grad_query, ((0,), (0,))).astype(low))

    pend = pending[0].reshape(2, SIZES["x"], rows_own, width)
    pend = jnp.where(h == 0, pend, pend[::-1])
    pend = jnp.transpose(pend, (1, 0, 2, 3)).reshape(tok, width)
    pend = join(columns(pend, c), swap(columns(pend, 1 - c), "c"))
    terms = dot(attended, wo, ((1,), (1,))).astype(low).astype(wide)
    hidden_out = (stream_f + collect_rows((pend.astype(wide) + terms).astype(low))).astype(low)

    grad_key = rotate(kv_grad[:, :HEAD_DIM].reshape(tok, 1, HEAD_DIM), -1.0)
    grad_kv = jnp.concatenate([grad_key.reshape(tok, HEAD_DIM), kv_grad[:, HEAD_DIM:]], axis=1)
    grad_kv = join_cores(grad_kv.astype(low))
    grad_w_kv = collect_yz(dot(normed, grad_kv, ((0,), (0,))).astype(low))
    normed_terms = dot(grad_query, wq, ((1,), (1,))) + dot(grad_kv, wkv, ((1,), (1,)))
    grad_normed = collect_rows(normed_terms.astype(low))

    kv_blocks = spread(grad_w_kv.astype(low), "x").astype(wide)
    kv_blocks = (kv_blocks[0::2] + kv_blocks[1::2]).astype(low)
    kv_other = swap(kv_blocks, "h")
    kv_blocks = jnp.concatenate(
        [jnp.where(h == 0, kv_blocks, kv_other), jnp.where(h == 0, kv_other, kv_blocks)], axis=0
    ).astype(wide)
    grad_k, grad_v = (
        jnp.transpose(kv_blocks[:, :, i : i + HEAD_DIM], (1, 0, 2)).reshape(k_weight.shape)
        for i in (0, HEAD_DIM)
    )

    gain_part = jnp.sum(q_weight.astype(wide) * grad_q, axis=1)
    gain_part = gain_part + jnp.sum(kv_weight.astype(wide) * grad_w_kv, axis=1)
    gain_part = jnp.sum(spread(gain_part, "x"), axis=0)
    gain_part = gain_part + swap(gain_part, "h")
    gain_half = spread_yz(gain_part[None])
    gain_other = swap(gain_half, "c")
    grad_gain = jnp.stack(
        [jnp.where(c == 0, gain_half, gain_other), jnp.where(c == 0, gain_other, gain_half)], axis=1
    ).reshape(width) / gain

    scaled_grad = grad_normed * gain
    grad_stream = (
        inv_rms
        * (scaled_grad - unit_rows * jnp.mean(scaled_grad * unit_rows, axis=-1, keepdims=True))
        + grad_out.astype(wide)
    ).astype(low)
    return (hidden_out, grad_stream, grad_gain, grad_q, grad_k, grad_v, grad_o)


def solution(mesh):
    fine = Mesh(mesh.devices.reshape(tuple(SIZES.values())), tuple(SIZES))
    whole = P(DP + TENSOR, None)
    in_specs = (
        whole,
        P(TENSOR, DP, None),
        P(),
        P(DP, TENSOR),
        P(DP, None),
        P(DP, None),
        P(DP, TENSOR),
        whole,
        P(),
    )
    out_specs = (whole, whole, P(), P(DP, TENSOR), P(DP, None), P(DP, None), P(DP, TENSOR))
    return jax.shard_map(
        on_device, mesh=fine, in_specs=in_specs, out_specs=out_specs, check_vma=False
    )
```

```python
import jax
import jax.numpy as jnp
from jax import lax
from jax.sharding import Mesh
from jax.sharding import PartitionSpec as P

HEADS = 32
KV_HEADS = 4
HEAD_DIM = 128
HALF_DIM = HEAD_DIM // 2

eps = 1e-05
rope_base = 500000.0

SIZES = {"y": 4, "z": 4, "c": 2, "h": 2, "x": 4}
DP = ("y", "z", "c")
TENSOR = ("h", "x")
NX = SIZES["x"]
wide = jnp.float32
low = jnp.bfloat16


def dot(a, b, dims):
    return lax.dot_general(a, b, (dims, ((), ())), preferred_element_type=wide)


def swap(a, axis):
    return lax.ppermute(a, axis, [(0, 1), (1, 0)])


def shift(a, step):
    return lax.ppermute(a, "x", [((i + step) % NX, i) for i in range(NX)])


def spread(a, axis):
    size = SIZES[axis]
    return lax.all_to_all(
        jnp.broadcast_to(a[None], (size,) + a.shape), axis, 0, 0, tiled=True
    )


def spread_yz(a):
    rows, cols = a.shape
    a = spread(a, "z").reshape(SIZES["z"] * rows, cols)
    return spread(a, "y").reshape(SIZES["y"] * SIZES["z"] * rows, cols)


def collect(a, axis):
    return jnp.sum(lax.all_to_all(a, axis, 0, 0, tiled=True).astype(wide), axis=0)


def collect_yz(a):
    rows, cols = a.shape
    a = collect(a.reshape(SIZES["y"], rows // SIZES["y"], cols), "y").astype(low)
    return collect(a.reshape(SIZES["z"], a.shape[0] // SIZES["z"], cols), "z")


def spread_tensor(a):
    both = jnp.stack([a, swap(a, "h")])
    return jnp.stack([both] + [shift(both, k) for k in range(1, NX)])


def collect_tensor(a):
    total = a[0].astype(wide)
    for k in range(1, NX):
        total = total + shift(a[k], NX - k).astype(wide)
    return total[0] + swap(total[1].astype(low), "h").astype(wide)


def on_device(
    stream_in, pending, gain, q_weight, k_weight, v_weight, out_weight, grad_out, doc_ids
):
    y, z, c, h, x = (lax.axis_index(a) for a in ("y", "z", "c", "h", "x"))
    tens_index = h * NX + x
    rows_own, width = stream_in.shape
    tok = pending.shape[1]
    outer = SIZES["y"] * SIZES["z"]
    n_dp = outer * 2
    block = width // n_dp
    q_width = q_weight.shape[1]
    heads = q_width // HEAD_DIM
    seq_len = doc_ids.shape[0]
    scale = HEAD_DIM ** (-0.5)

    def by_core(near):
        cols = near.shape[1]
        far = swap(near, "c")
        near, far = (a.reshape(outer, 1, near.shape[0] // outer, cols) for a in (near, far))
        pair = [jnp.where(c == 0, near, far), jnp.where(c == 0, far, near)]
        return jnp.concatenate(pair, axis=1).reshape(-1, cols)

    weights = lax.all_gather(
        jnp.concatenate([q_weight, out_weight], axis=1), DP, axis=0, tiled=True
    )
    wq, wo = weights[:, :q_width], weights[:, q_width:]

    kv_first = tens_index * heads // (HEADS // KV_HEADS) * HEAD_DIM
    kv_weight = jnp.concatenate(
        [lax.dynamic_slice_in_dim(w, kv_first, HEAD_DIM, 1) for w in (k_weight, v_weight)], axis=1
    )
    wkv = by_core(spread_yz(kv_weight))

    stream_f = stream_in.astype(wide)
    inv_rms = lax.rsqrt(jnp.mean(stream_f * stream_f, axis=-1, keepdims=True) + eps)
    unit_rows = stream_f * inv_rms
    normed_own = (unit_rows * gain).astype(low)
    normed = spread_tensor(normed_own).reshape(tok, width)

    def index(axis):
        return lax.broadcasted_iota(jnp.int32, (NX, 2, rows_own), axis)

    local = (((h ^ index(1)) * NX + (x + index(0)) % NX) * rows_own + index(2)).reshape(tok)
    block_first = ((y * SIZES["z"] + z) * 2 + c) * tok
    places = block_first + local
    rel_c = jnp.arange(2, dtype=jnp.int32)[:, None, None]
    at_yz = jnp.arange(outer, dtype=jnp.int32)[None, :, None]
    key_place = ((at_yz * 2 + (c ^ rel_c)) * tok + local[None, None, :]).reshape(seq_len)

    def relative(a):
        a = a.reshape((2, NX, rows_own) + a.shape[1:])
        a = jnp.where(h == 0, a, a[::-1])
        a = lax.dynamic_slice_in_dim(jnp.concatenate([a, a], axis=1), x, NX, 1)
        return jnp.swapaxes(a, 0, 1)

    doc_query = relative(lax.dynamic_slice_in_dim(doc_ids, block_first, tok)).reshape(tok)
    first_place = jnp.sum((doc_ids[None, :] < doc_query[:, None]).astype(jnp.int32), axis=1)
    allowed = (key_place[None, :] <= places[:, None]) & (key_place[None, :] >= first_place[:, None])

    frequency = rope_base ** (-2.0 * jnp.arange(HALF_DIM).astype(wide) / HEAD_DIM)
    angles = places.astype(wide)[:, None] * frequency[None, :]
    cosine, sine = jnp.cos(angles)[:, None, :], jnp.sin(angles)[:, None, :]

    def rotate(field, sign):
        first, second = field[..., :HALF_DIM], field[..., HALF_DIM:]
        return jnp.concatenate(
            [first * cosine - sign * second * sine, second * cosine + sign * first * sine], axis=-1
        )

    kv_proj = dot(normed, wkv, ((1,), (0,)))
    keys_own = rotate(kv_proj[:, :HEAD_DIM].reshape(tok, 1, HEAD_DIM), 1.0).reshape(tok, HEAD_DIM)
    kv_own = jnp.concatenate([keys_own, kv_proj[:, HEAD_DIM:]], axis=1).astype(low)
    kv_near = spread_yz(kv_own)
    kv_all = jnp.concatenate([kv_near, swap(kv_near, "c")], axis=0)
    keys, values = kv_all[:, :HEAD_DIM], kv_all[:, HEAD_DIM:]

    grads = spread_tensor(grad_out).reshape(tok, width)

    both_own = jnp.stack([normed_own, grad_out]).reshape(2, rows_own, n_dp, block)
    both_own = lax.all_to_all(jnp.transpose(both_own, (2, 0, 1, 3)), DP, 0, 0, tiled=True)
    both_rows = jnp.transpose(spread_tensor(both_own), (3, 2, 0, 1, 4, 5))
    normed_rows, grad_rows = (both_rows[i].reshape(seq_len, block) for i in range(2))
    normed_cores = normed_rows.reshape(outer, 2, tok, block)

    query = rotate(dot(normed, wq, ((1,), (0,))).reshape(tok, heads, HEAD_DIM), 1.0).astype(low)
    query = jnp.transpose(query, (1, 0, 2)).reshape(heads * tok, HEAD_DIM)
    grad_heads = dot(grads, wo, ((1,), (0,))).astype(low)
    grad_heads = jnp.transpose(grad_heads.reshape(tok, heads, HEAD_DIM), (1, 0, 2))
    grad_heads = grad_heads.reshape(heads * tok, HEAD_DIM)

    scores = dot(query, keys, ((1,), (1,))).reshape(heads, tok, seq_len) * scale
    scores = jnp.where(allowed[None], scores, -1e30)
    peak = jnp.max(scores, axis=-1, keepdims=True)
    exp_terms = jnp.exp(scores - peak)
    prob = (exp_terms / jnp.sum(exp_terms, axis=-1, keepdims=True)).reshape(heads * tok, seq_len)
    prob_low = prob.astype(low)
    attended_h = dot(prob_low, values, ((1,), (0,))).astype(low)
    attended = jnp.transpose(attended_h.reshape(heads, tok, HEAD_DIM), (1, 0, 2))
    attended = attended.reshape(tok, q_width)

    delta = jnp.sum(grad_heads.astype(wide) * attended_h.astype(wide), axis=-1, keepdims=True)
    grad_prob = dot(grad_heads, values, ((1,), (1,)))
    grad_score = (prob * (grad_prob - delta)).astype(low)
    grad_query = (dot(grad_score, keys, ((1,), (0,))) * scale).reshape(heads, tok, HEAD_DIM)
    grad_query = rotate(jnp.transpose(grad_query, (1, 0, 2)), -1.0).astype(low)
    grad_query = grad_query.reshape(tok, q_width)
    att_gq = lax.all_gather(
        jnp.concatenate([attended, grad_query], axis=1), DP, axis=0, tiled=True
    )
    grad_o = dot(grad_rows, att_gq[:, :q_width], ((0,), (0,)))
    grad_q = dot(normed_rows, att_gq[:, q_width:], ((0,), (0,)))

    key_piece = dot(grad_score, query, ((0,), (0,))) * scale
    value_piece = dot(prob_low, grad_heads, ((0,), (0,)))
    kv_piece = jnp.concatenate([key_piece, value_piece], axis=1).astype(low)
    kv_sum = kv_piece[: seq_len // 2].astype(wide) + swap(kv_piece[seq_len // 2 :], "c").astype(wide)
    kv_grad = collect_yz(kv_sum.astype(low))
    grad_key = rotate(kv_grad[:, :HEAD_DIM].reshape(tok, 1, HEAD_DIM), -1.0)
    grad_kv = jnp.concatenate([grad_key.reshape(tok, HEAD_DIM), kv_grad[:, HEAD_DIM:]], axis=1)
    grad_kv = grad_kv.astype(low)

    gkv_near = spread_yz(grad_kv)
    gkv_far = swap(gkv_near, "c")
    rows_near, rows_far = (
        lax.dynamic_index_in_dim(normed_cores, i, 1, keepdims=False).reshape(-1, block)
        for i in (c, 1 - c)
    )
    grad_w_kv = dot(rows_near, gkv_near, ((0,), (0,))) + dot(rows_far, gkv_far, ((0,), (0,)))

    terms = dot(attended, wo, ((1,), (1,))).astype(low).astype(wide)
    terms = terms.reshape(NX, 2, rows_own, width) + relative(pending[0]).astype(wide)
    hidden_out = (stream_f + collect_tensor(terms.astype(low))).astype(low)

    normed_terms = dot(grad_query, wq, ((1,), (1,))) + dot(grad_kv, wkv, ((1,), (1,)))
    grad_normed = collect_tensor(normed_terms.astype(low).reshape(NX, 2, rows_own, width))

    kv_own_w = grad_w_kv.astype(low)
    kv_blocks = [kv_own_w.astype(wide)] + [shift(kv_own_w, k).astype(wide) for k in range(1, NX)]
    odd = x % 2 == 1
    near = kv_blocks[0] + jnp.where(odd, kv_blocks[3], kv_blocks[1])
    far = kv_blocks[2] + jnp.where(odd, kv_blocks[1], kv_blocks[3])
    pair = jnp.stack([jnp.where(x < 2, near, far), jnp.where(x < 2, far, near)]).astype(low)
    other = swap(pair, "h")
    pair = jnp.concatenate(
        [jnp.where(h == 0, pair, other), jnp.where(h == 0, other, pair)], axis=0
    ).astype(wide)
    grad_k, grad_v = (
        jnp.transpose(pair[:, :, i : i + HEAD_DIM], (1, 0, 2)).reshape(k_weight.shape)
        for i in (0, HEAD_DIM)
    )

    gain_part = jnp.sum(q_weight.astype(wide) * grad_q, axis=1)
    gain_part = gain_part + jnp.sum(kv_weight.astype(wide) * grad_w_kv, axis=1)
    gain_part = gain_part + sum(shift(gain_part, k) for k in range(1, NX))
    gain_part = gain_part + swap(gain_part, "h")
    grad_gain = by_core(spread_yz(gain_part[None])).reshape(width) / gain

    scaled_grad = grad_normed * gain
    grad_stream = (
        inv_rms
        * (scaled_grad - unit_rows * jnp.mean(scaled_grad * unit_rows, axis=-1, keepdims=True))
        + grad_out.astype(wide)
    ).astype(low)
    return (hidden_out, grad_stream, grad_gain, grad_q, grad_k, grad_v, grad_o)


def solution(mesh):
    fine = Mesh(mesh.devices.reshape(tuple(SIZES.values())), tuple(SIZES))
    whole = P(DP + TENSOR, None)
    in_specs = (
        whole,
        P(TENSOR, DP, None),
        P(),
        P(DP, TENSOR),
        P(DP, None),
        P(DP, None),
        P(DP, TENSOR),
        whole,
        P(),
    )
    out_specs = (whole, whole, P(), P(DP, TENSOR), P(DP, None), P(DP, None), P(DP, TENSOR))
    return jax.shard_map(
        on_device, mesh=fine, in_specs=in_specs, out_specs=out_specs, check_vma=False
    )
```

```python
import jax
import jax.numpy as jnp
from jax import lax
from jax.experimental import pallas as pl
from jax.experimental.pallas import tpu as pltpu
from jax.sharding import Mesh
from jax.sharding import PartitionSpec as P

HEADS = 32
KV_HEADS = 4
HEAD_DIM = 128
HALF_DIM = HEAD_DIM // 2

eps = 1e-05
rope_base = 500000.0

SIZES = {"y": 4, "z": 4, "c": 2, "h": 2, "x": 4}
DP = ("y", "z", "c")
TENSOR = ("h", "x")
NX = SIZES["x"]
wide = jnp.float32
low = jnp.bfloat16


def dot(a, b, dims):
    return lax.dot_general(a, b, (dims, ((), ())), preferred_element_type=wide)


def swap(a, axis):
    return lax.ppermute(a, axis, [(0, 1), (1, 0)])


def shift(a, step):
    return lax.ppermute(a, "x", [((i + step) % NX, i) for i in range(NX)])


def spread(a, axis):
    size = SIZES[axis]
    return lax.all_to_all(
        jnp.broadcast_to(a[None], (size,) + a.shape), axis, 0, 0, tiled=True
    )


def spread_yz(a):
    rows, cols = a.shape
    a = spread(a, "z").reshape(SIZES["z"] * rows, cols)
    return spread(a, "y").reshape(SIZES["y"] * SIZES["z"] * rows, cols)


def collect(a, axis):
    return jnp.sum(lax.all_to_all(a, axis, 0, 0, tiled=True).astype(wide), axis=0)


def collect_yz(a):
    rows, cols = a.shape
    a = collect(a.reshape(SIZES["y"], rows // SIZES["y"], cols), "y").astype(low)
    return collect(a.reshape(SIZES["z"], a.shape[0] // SIZES["z"], cols), "z")


def all_sum(a, axis):
    if SIZES[axis] == 2:
        return a + swap(a, axis)
    far = [lax.ppermute(a, axis, [(i, i ^ k) for i in range(4)]) for k in range(1, 4)]
    return (a + far[0]) + (far[1] + far[2])


def spread_tensor(a):
    both = jnp.stack([a, swap(a, "h")])
    return jnp.stack([both] + [shift(both, k) for k in range(1, NX)])


def collect_tensor(a):
    total = a[0].astype(wide)
    for k in range(1, NX):
        total = total + shift(a[k], NX - k).astype(wide)
    return total[0] + swap(total[1].astype(low), "h").astype(wide)


def turn(field, cosine, sine):
    return field * cosine + pltpu.roll(field, HALF_DIM, 1) * sine


PARAMS = pltpu.CompilerParams(vmem_limit_bytes=48 * 2**20)
ANY = pl.BlockSpec(memory_space=pl.ANY)


def project_kernel(normed, grads, weights, cosine, sine, rows, pend, query, grad_heads, total):
    step = pl.program_id(0)
    tok, half = normed.shape[0], weights.shape[1] // 2

    @pl.when(step == 0)
    def _():
        total[...] = jnp.zeros_like(total)

    total[:, :half] += dot(normed[...], weights[:, :half], ((1,), (0,)))
    total[:, half:] += dot(grads[...], weights[:, half:], ((1,), (0,)))

    @pl.when(step == pl.num_programs(0) - 1)
    def _():
        for i in range(half // HEAD_DIM):
            at = pl.ds(i * tok, tok)
            query[at, :] = turn(
                total[:, i * HEAD_DIM : (i + 1) * HEAD_DIM], cosine[...], sine[...]
            ).astype(low)
            grad_heads[at, :] = total[
                :, half + i * HEAD_DIM : half + (i + 1) * HEAD_DIM
            ].astype(low)


def project(normed, grads, weights, cosine, sine, rows, pend, step=512):
    tok, width = normed.shape
    cols = weights.shape[1]
    out = jax.ShapeDtypeStruct((cols // 2 // HEAD_DIM * tok, HEAD_DIM), low)
    fixed = pl.BlockSpec((tok, HEAD_DIM), lambda i: (0, 0))
    return pl.pallas_call(
        project_kernel,
        grid=(width // step,),
        in_specs=[
            pl.BlockSpec((tok, step), lambda i: (0, i)),
            pl.BlockSpec((tok, step), lambda i: (0, i)),
            pl.BlockSpec((step, cols), lambda i: (i, 0)),
            fixed,
            fixed,
            ANY,
            ANY,
        ],
        out_specs=[pl.BlockSpec(out.shape, lambda i: (0, 0))] * 2,
        out_shape=[out, out],
        scratch_shapes=[pltpu.VMEM((tok, cols), wide)],
        compiler_params=PARAMS,
    )(normed, grads, weights, cosine, sine, rows, pend)


def attend_kernel(
    query, grad_heads, near, far, key_place, bounds, cosine, sine, att_gq, near_grad, far_grad, score
):
    rows = query.shape[0]
    tok = cosine.shape[0]
    heads = rows // tok
    half = near.shape[0]
    step = 512
    scale = HEAD_DIM ** (-0.5)
    q, g = query[...], grad_heads[...]
    last, first = bounds[0:1, :], bounds[1:2, :]

    peak = jnp.full((1, rows), -1e30, wide)
    for kv, base in ((near, 0), (far, half)):

        def mark(i, peak, kv=kv, base=base):
            at = pl.multiple_of(i * step, step)
            s = dot(kv[pl.ds(at, step), :HEAD_DIM], q, ((1,), (1,))) * scale
            place = key_place[pl.ds(base + at, step), :]
            place = jnp.broadcast_to(place, (step, tok))
            bias = jnp.where((place <= last) & (place >= first), 0.0, -1e30)
            s = s + jnp.concatenate([bias] * heads, axis=1)
            score[pl.ds(base + at, step), :] = s
            return jnp.maximum(peak, jnp.max(s, axis=0, keepdims=True))

        peak = lax.fori_loop(0, half // step, mark, peak)

    carry = (jnp.zeros((1, rows), wide), jnp.zeros((HEAD_DIM, rows), wide))
    for kv, base in ((near, 0), (far, half)):

        def weigh(i, carry, kv=kv, base=base):
            norm, out = carry
            at = pl.multiple_of(i * step, step)
            e = jnp.exp(score[pl.ds(base + at, step), :] - peak)
            score[pl.ds(base + at, step), :] = e
            out = out + dot(kv[pl.ds(at, step), HEAD_DIM:], e.astype(low), ((0,), (0,)))
            return norm + jnp.sum(e, axis=0, keepdims=True), out

        carry = lax.fori_loop(0, half // step, weigh, carry)
    norm, out = carry
    inverse = 1.0 / norm
    out = (out * inverse).astype(low).astype(wide)
    delta = jnp.sum(out * g.astype(wide).T, axis=0, keepdims=True)

    grad_query = jnp.zeros((HEAD_DIM, rows), wide)
    for kv, grad, base in ((near, near_grad, 0), (far, far_grad, half)):

        def back(i, grad_query, kv=kv, grad=grad, base=base):
            at = pl.multiple_of(i * step, step)
            p = score[pl.ds(base + at, step), :] * inverse
            gp = dot(kv[pl.ds(at, step), HEAD_DIM:], g, ((1,), (1,)))
            gs = (p * (gp - delta)).astype(low)
            grad[pl.ds(at, step), :HEAD_DIM] = (dot(gs, q, ((1,), (0,))) * scale).astype(low)
            grad[pl.ds(at, step), HEAD_DIM:] = dot(p.astype(low), g, ((1,), (0,))).astype(low)
            return grad_query + dot(kv[pl.ds(at, step), :HEAD_DIM], gs, ((0,), (0,)))

        grad_query = lax.fori_loop(0, half // step, back, grad_query)

    for i in range(heads):
        at, cols = slice(i * tok, (i + 1) * tok), slice(i * HEAD_DIM, (i + 1) * HEAD_DIM)
        att_gq[:, cols] = out[:, at].T.astype(low)
        back_cols = slice(heads * HEAD_DIM + cols.start, heads * HEAD_DIM + cols.stop)
        att_gq[:, back_cols] = turn(
            grad_query[:, at].T * scale, cosine[...], -sine[...]
        ).astype(low)


def attend(query, grad_heads, near, far, key_place, bounds, cosine, sine):
    rows, tok = query.shape[0], cosine.shape[0]
    half = near.shape[0]
    return pl.pallas_call(
        attend_kernel,
        out_shape=[
            jax.ShapeDtypeStruct((tok, 2 * rows // tok * HEAD_DIM), low),
            jax.ShapeDtypeStruct(near.shape, low),
            jax.ShapeDtypeStruct(far.shape, low),
        ],
        scratch_shapes=[pltpu.VMEM((2 * half, rows), wide)],
        compiler_params=PARAMS,
    )(query, grad_heads, near, far, key_place, bounds, cosine, sine)


def back_project_kernel(att_gq, weights, terms, grad):
    half = weights.shape[1] // 2
    terms[...] = dot(att_gq[:, :half], weights[:, half:], ((1,), (1,))).astype(low)
    grad[...] = dot(att_gq[:, half:], weights[:, :half], ((1,), (1,)))


def back_project(att_gq, weights, step=512):
    tok = att_gq.shape[0]
    width, cols = weights.shape
    out = pl.BlockSpec((tok, step), lambda i: (0, i))
    return pl.pallas_call(
        back_project_kernel,
        grid=(width // step,),
        in_specs=[
            pl.BlockSpec(att_gq.shape, lambda i: (0, 0)),
            pl.BlockSpec((step, cols), lambda i: (i, 0)),
        ],
        out_specs=[out, out],
        out_shape=[
            jax.ShapeDtypeStruct((tok, width), low),
            jax.ShapeDtypeStruct((tok, width), wide),
        ],
        compiler_params=PARAMS,
    )(att_gq, weights)


def weight_grad_kernel(rows, att_gq, grad_o, grad_q):
    half, block = att_gq.shape[1] // 2, rows.shape[1] // 2

    @pl.when(pl.program_id(0) == 0)
    def _():
        grad_o[...] = jnp.zeros_like(grad_o)
        grad_q[...] = jnp.zeros_like(grad_q)

    grad_o[...] += dot(rows[:, :block], att_gq[:, :half], ((0,), (0,)))
    grad_q[...] += dot(rows[:, block:], att_gq[:, half:], ((0,), (0,)))


def weight_grads(rows, att_gq, step=512):
    seq_len, cols = att_gq.shape
    out = jax.ShapeDtypeStruct((rows.shape[1] // 2, cols // 2), wide)
    return pl.pallas_call(
        weight_grad_kernel,
        grid=(seq_len // step,),
        in_specs=[
            pl.BlockSpec((step, rows.shape[1]), lambda i: (i, 0)),
            pl.BlockSpec((step, cols), lambda i: (i, 0)),
        ],
        out_specs=[pl.BlockSpec(out.shape, lambda i: (0, 0))] * 2,
        out_shape=[out, out],
        compiler_params=PARAMS,
    )(rows, att_gq)


def on_device(
    stream_in, pending, gain, q_weight, k_weight, v_weight, out_weight, grad_out, doc_ids
):
    y, z, c, h, x = (lax.axis_index(a) for a in ("y", "z", "c", "h", "x"))
    tens_index = h * NX + x
    rows_own, width = stream_in.shape
    tok = pending.shape[1]
    outer = SIZES["y"] * SIZES["z"]
    n_dp = outer * 2
    block = width // n_dp
    q_width = q_weight.shape[1]
    seq_len = doc_ids.shape[0]

    def by_core(near):
        cols = near.shape[1]
        far = swap(near, "c")
        near, far = (a.reshape(outer, 1, near.shape[0] // outer, cols) for a in (near, far))
        pair = [jnp.where(c == 0, near, far), jnp.where(c == 0, far, near)]
        return jnp.concatenate(pair, axis=1).reshape(-1, cols)

    weights = lax.all_gather(
        jnp.concatenate([q_weight, out_weight], axis=1), DP, axis=0, tiled=True
    )

    kv_first = tens_index * (q_width // HEAD_DIM) // (HEADS // KV_HEADS) * HEAD_DIM
    kv_weight = jnp.concatenate(
        [lax.dynamic_slice_in_dim(w, kv_first, HEAD_DIM, 1) for w in (k_weight, v_weight)], axis=1
    )
    wkv = by_core(spread_yz(kv_weight))

    stream_f = stream_in.astype(wide)
    inv_rms = lax.rsqrt(jnp.mean(stream_f * stream_f, axis=-1, keepdims=True) + eps)
    unit_rows = stream_f * inv_rms
    normed_own = (unit_rows * gain).astype(low)
    normed = spread_tensor(normed_own).reshape(tok, width)

    def index(axis):
        return lax.broadcasted_iota(jnp.int32, (NX, 2, rows_own), axis)

    local = (((h ^ index(1)) * NX + (x + index(0)) % NX) * rows_own + index(2)).reshape(tok)
    block_first = ((y * SIZES["z"] + z) * 2 + c) * tok
    places = block_first + local
    rel_c = jnp.arange(2, dtype=jnp.int32)[:, None, None]
    at_yz = jnp.arange(outer, dtype=jnp.int32)[None, :, None]
    key_place = ((at_yz * 2 + (c ^ rel_c)) * tok + local[None, None, :]).reshape(seq_len, 1)

    def relative(a):
        a = a.reshape((2, NX, rows_own) + a.shape[1:])
        a = jnp.where(h == 0, a, a[::-1])
        a = lax.dynamic_slice_in_dim(jnp.concatenate([a, a], axis=1), x, NX, 1)
        return jnp.swapaxes(a, 0, 1)

    doc_query = relative(lax.dynamic_slice_in_dim(doc_ids, block_first, tok)).reshape(tok)
    first_place = jnp.sum((doc_ids[None, :] < doc_query[:, None]).astype(jnp.int32), axis=1)

    frequency = rope_base ** (-2.0 * jnp.arange(HALF_DIM).astype(wide) / HEAD_DIM)
    angles = places.astype(wide)[:, None] * frequency[None, :]
    cosine, sine = jnp.cos(angles), jnp.sin(angles)
    cosine = jnp.concatenate([cosine, cosine], axis=1)
    sine = jnp.concatenate([-sine, sine], axis=1)

    def rotate(field, sign):
        flipped = jnp.concatenate([field[:, HALF_DIM:], field[:, :HALF_DIM]], axis=1)
        return field * cosine + sign * flipped * sine

    kv_proj = dot(normed, wkv, ((1,), (0,)))
    keys_own = rotate(kv_proj[:, :HEAD_DIM], 1.0)
    kv_own = jnp.concatenate([keys_own, kv_proj[:, HEAD_DIM:]], axis=1).astype(low)
    kv_near = spread_yz(kv_own)
    kv_far = swap(kv_near, "c")

    grads = spread_tensor(grad_out).reshape(tok, width)

    split = [a.reshape(rows_own, n_dp, block) for a in (grad_out, normed_own)]
    rows = jnp.transpose(jnp.concatenate(split, axis=2), (1, 0, 2))
    rows = spread_tensor(lax.all_to_all(rows, DP, 0, 0, tiled=True))
    rows = jnp.transpose(rows, (2, 0, 1, 3, 4)).reshape(seq_len, 2 * block)
    normed_cores = rows[:, block:].reshape(outer, 2, tok, block)
    rows_near, rows_far = (
        lax.dynamic_index_in_dim(normed_cores, i, 1, keepdims=False).reshape(-1, block)
        for i in (c, 1 - c)
    )
    pend = relative(pending[0])

    query, grad_heads = project(normed, grads, weights, cosine, sine, rows, pend)
    bounds = jnp.stack([places, first_place])
    att_gq, near_piece, far_piece = attend(
        query, grad_heads, kv_near, kv_far, key_place, bounds, cosine, sine
    )
    att_gq_all = lax.all_gather(att_gq, DP, axis=0, tiled=True)

    kv_sum = near_piece.astype(wide) + swap(far_piece, "c").astype(wide)
    kv_grad = collect_yz(kv_sum.astype(low))
    grad_key = rotate(kv_grad[:, :HEAD_DIM], -1.0)
    grad_kv = jnp.concatenate([grad_key, kv_grad[:, HEAD_DIM:]], axis=1).astype(low)

    gkv_near = spread_yz(grad_kv)
    gkv_far = swap(gkv_near, "c")
    grad_w_kv = dot(rows_near, gkv_near, ((0,), (0,))) + dot(rows_far, gkv_far, ((0,), (0,)))

    terms, query_terms = back_project(att_gq, weights)
    terms = terms.reshape(NX, 2, rows_own, width).astype(wide) + pend.astype(wide)
    hidden_out = (stream_f + collect_tensor(terms.astype(low))).astype(low)

    normed_terms = query_terms + dot(grad_kv, wkv, ((1,), (1,)))
    grad_normed = collect_tensor(normed_terms.astype(low).reshape(NX, 2, rows_own, width))
    gain_sum = jnp.sum(normed_terms * normed.astype(wide), axis=0).reshape(n_dp, block)
    for axis in ("c", "h", "x", "y", "z"):
        gain_sum = all_sum(gain_sum, axis)
    grad_gain = gain_sum.reshape(width) / gain

    grad_o, grad_q = weight_grads(rows, att_gq_all)

    kv_own_w = grad_w_kv.astype(low)
    kv_blocks = [kv_own_w.astype(wide)] + [shift(kv_own_w, k).astype(wide) for k in range(1, NX)]
    odd = x % 2 == 1
    near = kv_blocks[0] + jnp.where(odd, kv_blocks[3], kv_blocks[1])
    far = kv_blocks[2] + jnp.where(odd, kv_blocks[1], kv_blocks[3])
    pair = jnp.stack([jnp.where(x < 2, near, far), jnp.where(x < 2, far, near)]).astype(low)
    other = swap(pair, "h")
    pair = jnp.concatenate(
        [jnp.where(h == 0, pair, other), jnp.where(h == 0, other, pair)], axis=0
    ).astype(wide)
    grad_k, grad_v = (
        jnp.transpose(pair[:, :, i : i + HEAD_DIM], (1, 0, 2)).reshape(k_weight.shape)
        for i in (0, HEAD_DIM)
    )

    scaled_grad = grad_normed * gain
    grad_stream = (
        inv_rms
        * (scaled_grad - unit_rows * jnp.mean(scaled_grad * unit_rows, axis=-1, keepdims=True))
        + grad_out.astype(wide)
    ).astype(low)
    return (hidden_out, grad_stream, grad_gain, grad_q, grad_k, grad_v, grad_o)


def solution(mesh):
    fine = Mesh(mesh.devices.reshape(tuple(SIZES.values())), tuple(SIZES))
    whole = P(DP + TENSOR, None)
    in_specs = (
        whole,
        P(TENSOR, DP, None),
        P(),
        P(DP, TENSOR),
        P(DP, None),
        P(DP, None),
        P(DP, TENSOR),
        whole,
        P(),
    )
    out_specs = (whole, whole, P(), P(DP, TENSOR), P(DP, None), P(DP, None), P(DP, TENSOR))
    return jax.shard_map(
        on_device, mesh=fine, in_specs=in_specs, out_specs=out_specs, check_vma=False
    )
```

```python
import jax
import jax.numpy as jnp
from jax import lax
from jax.experimental import pallas as pl
from jax.experimental.pallas import tpu as pltpu
from jax.sharding import Mesh
from jax.sharding import PartitionSpec as P

HEADS = 32
KV_HEADS = 4
HEAD_DIM = 128
HALF_DIM = HEAD_DIM // 2

eps = 1e-05
rope_base = 500000.0

SIZES = {"y": 4, "z": 4, "c": 2, "h": 2, "x": 4}
DP = ("y", "z", "c")
TENSOR = ("h", "x")
NX = SIZES["x"]
wide = jnp.float32
low = jnp.bfloat16


def dot(a, b, dims):
    return lax.dot_general(a, b, (dims, ((), ())), preferred_element_type=wide)


def swap(a, axis):
    return lax.ppermute(a, axis, [(0, 1), (1, 0)])


def shift(a, step):
    return lax.ppermute(a, "x", [((i + step) % NX, i) for i in range(NX)])


def spread(a, axis):
    size = SIZES[axis]
    return lax.all_to_all(
        jnp.broadcast_to(a[None], (size,) + a.shape), axis, 0, 0, tiled=True
    )


def spread_yz(a):
    rows, cols = a.shape
    a = spread(a, "z").reshape(SIZES["z"] * rows, cols)
    return spread(a, "y").reshape(SIZES["y"] * SIZES["z"] * rows, cols)


def collect(a, axis):
    return jnp.sum(lax.all_to_all(a, axis, 0, 0, tiled=True).astype(wide), axis=0)


def all_sum(a, axis):
    if SIZES[axis] == 2:
        return a + swap(a, axis)
    far = [lax.ppermute(a, axis, [(i, i ^ k) for i in range(4)]) for k in range(1, 4)]
    return (a + far[0]) + (far[1] + far[2])


def spread_tensor(a):
    both = jnp.stack([a, swap(a, "h")])
    return jnp.stack([both] + [shift(both, k) for k in range(1, NX)])


def collect_tensor(a):
    total = a[0].astype(wide)
    for k in range(1, NX):
        total = total + shift(a[k], NX - k).astype(wide)
    return total[0] + swap(total[1].astype(low), "h").astype(wide)


def turn(field, cosine, sine):
    return field * cosine + pltpu.roll(field, HALF_DIM, 1) * sine


PARAMS = pltpu.CompilerParams(vmem_limit_bytes=48 * 2**20)
ANY = pl.BlockSpec(memory_space=pl.ANY)


def kv_project_kernel(both, weights, cosine, sine, rows, pend, kv, total):
    step = pl.program_id(0)

    @pl.when(step == 0)
    def _():
        total[...] = jnp.zeros_like(total)

    total[...] += dot(both[...], weights[...], ((1,), (0,)))

    @pl.when(step == pl.num_programs(0) - 1)
    def _():
        kv[:, :HEAD_DIM] = turn(total[:, :HEAD_DIM], cosine[...], sine[...]).astype(low)
        kv[:, HEAD_DIM:] = total[:, HEAD_DIM:].astype(low)


def kv_project(both, weights, cosine, sine, rows, pend, step=1024):
    tok = both.shape[0]
    width, cols = weights.shape
    kv_cols = 2 * HEAD_DIM
    fixed = pl.BlockSpec((tok, HEAD_DIM), lambda i: (0, 0))
    return pl.pallas_call(
        kv_project_kernel,
        grid=(width // step,),
        in_specs=[
            pl.BlockSpec((tok, step), lambda i: (0, i)),
            pl.BlockSpec((step, kv_cols), lambda i: (i, cols // kv_cols - 1)),
            fixed,
            fixed,
            ANY,
            ANY,
        ],
        out_specs=pl.BlockSpec((tok, kv_cols), lambda i: (0, 0)),
        out_shape=jax.ShapeDtypeStruct((tok, kv_cols), low),
        scratch_shapes=[pltpu.VMEM((tok, kv_cols), wide)],
        compiler_params=PARAMS,
    )(both, weights, cosine, sine, rows, pend)


def project_kernel(normed, grads, weights, cosine, sine, query, grad_heads, total):
    step = pl.program_id(0)
    tok, half = normed.shape[0], weights.shape[1] // 2

    @pl.when(step == 0)
    def _():
        total[...] = jnp.zeros_like(total)

    total[:, :half] += dot(normed[...], weights[:, :half], ((1,), (0,)))
    total[:, half:] += dot(grads[...], weights[:, half:], ((1,), (0,)))

    @pl.when(step == pl.num_programs(0) - 1)
    def _():
        for i in range(half // HEAD_DIM):
            at = pl.ds(i * tok, tok)
            query[at, :] = turn(
                total[:, i * HEAD_DIM : (i + 1) * HEAD_DIM], cosine[...], sine[...]
            ).astype(low)
            grad_heads[at, :] = total[
                :, half + i * HEAD_DIM : half + (i + 1) * HEAD_DIM
            ].astype(low)


def project(both, weights, cosine, sine, cols, step=512):
    tok = both.shape[0]
    width = weights.shape[0]
    steps = width // step
    out = jax.ShapeDtypeStruct((cols // 2 // HEAD_DIM * tok, HEAD_DIM), low)
    fixed = pl.BlockSpec((tok, HEAD_DIM), lambda i: (0, 0))
    return pl.pallas_call(
        project_kernel,
        grid=(steps,),
        in_specs=[
            pl.BlockSpec((tok, step), lambda i: (0, i)),
            pl.BlockSpec((tok, step), lambda i: (0, i + steps)),
            pl.BlockSpec((step, cols), lambda i: (i, 0)),
            fixed,
            fixed,
        ],
        out_specs=[pl.BlockSpec(out.shape, lambda i: (0, 0))] * 2,
        out_shape=[out, out],
        scratch_shapes=[pltpu.VMEM((tok, cols), wide)],
        compiler_params=PARAMS,
    )(both, both, weights, cosine, sine)


def hold_kernel(value, other, out):
    out[...] = value[...]


def hold(value, other):
    return pl.pallas_call(
        hold_kernel,
        in_specs=[pl.BlockSpec(memory_space=pltpu.VMEM), ANY],
        out_shape=jax.ShapeDtypeStruct(value.shape, value.dtype),
    )(value, other)


def attend_kernel(
    query, grad_heads, near, far, key_place, bounds, cosine, sine, att_gq, near_grad, far_grad, score
):
    rows = query.shape[0]
    tok = cosine.shape[0]
    heads = rows // tok
    half = near.shape[0]
    step = 512
    scale = HEAD_DIM ** (-0.5)
    q, g = query[...], grad_heads[...]
    last, first = bounds[0:1, :], bounds[1:2, :]

    peak = jnp.full((1, rows), -1e30, wide)
    for kv, base in ((near, 0), (far, half)):

        def mark(i, peak, kv=kv, base=base):
            at = pl.multiple_of(i * step, step)
            s = dot(kv[pl.ds(at, step), :HEAD_DIM], q, ((1,), (1,))) * scale
            place = key_place[pl.ds(base + at, step), :]
            place = jnp.broadcast_to(place, (step, tok))
            bias = jnp.where((place <= last) & (place >= first), 0.0, -1e30)
            s = s + jnp.concatenate([bias] * heads, axis=1)
            score[pl.ds(base + at, step), :] = s
            return jnp.maximum(peak, jnp.max(s, axis=0, keepdims=True))

        peak = lax.fori_loop(0, half // step, mark, peak)

    carry = (jnp.zeros((1, rows), wide), jnp.zeros((HEAD_DIM, rows), wide))
    for kv, base in ((near, 0), (far, half)):

        def weigh(i, carry, kv=kv, base=base):
            norm, out = carry
            at = pl.multiple_of(i * step, step)
            e = jnp.exp(score[pl.ds(base + at, step), :] - peak)
            score[pl.ds(base + at, step), :] = e
            out = out + dot(kv[pl.ds(at, step), HEAD_DIM:], e.astype(low), ((0,), (0,)))
            return norm + jnp.sum(e, axis=0, keepdims=True), out

        carry = lax.fori_loop(0, half // step, weigh, carry)
    norm, out = carry
    inverse = 1.0 / norm
    out = (out * inverse).astype(low).astype(wide)
    delta = jnp.sum(out * g.astype(wide).T, axis=0, keepdims=True)

    grad_query = jnp.zeros((HEAD_DIM, rows), wide)
    for kv, grad, base in ((near, near_grad, 0), (far, far_grad, half)):

        def back(i, grad_query, kv=kv, grad=grad, base=base):
            at = pl.multiple_of(i * step, step)
            p = score[pl.ds(base + at, step), :] * inverse
            gp = dot(kv[pl.ds(at, step), HEAD_DIM:], g, ((1,), (1,)))
            gs = (p * (gp - delta)).astype(low)
            grad[pl.ds(at, step), :HEAD_DIM] = (dot(gs, q, ((1,), (0,))) * scale).astype(low)
            grad[pl.ds(at, step), HEAD_DIM:] = dot(p.astype(low), g, ((1,), (0,))).astype(low)
            return grad_query + dot(kv[pl.ds(at, step), :HEAD_DIM], gs, ((0,), (0,)))

        grad_query = lax.fori_loop(0, half // step, back, grad_query)

    for i in range(heads):
        at, cols = slice(i * tok, (i + 1) * tok), slice(i * HEAD_DIM, (i + 1) * HEAD_DIM)
        att_gq[:, cols] = out[:, at].T.astype(low)
        back_cols = slice(heads * HEAD_DIM + cols.start, heads * HEAD_DIM + cols.stop)
        att_gq[:, back_cols] = turn(
            grad_query[:, at].T * scale, cosine[...], -sine[...]
        ).astype(low)


def attend(query, grad_heads, near, far, key_place, bounds, cosine, sine):
    rows, tok = query.shape[0], cosine.shape[0]
    half = near.shape[0]
    return pl.pallas_call(
        attend_kernel,
        out_shape=[
            jax.ShapeDtypeStruct((tok, 2 * rows // tok * HEAD_DIM), low),
            jax.ShapeDtypeStruct(near.shape, low),
            jax.ShapeDtypeStruct(far.shape, low),
        ],
        scratch_shapes=[pltpu.VMEM((2 * half, rows), wide)],
        compiler_params=PARAMS,
    )(query, grad_heads, near, far, key_place, bounds, cosine, sine)


def back_project_kernel(att_gq, weights, terms, grad):
    half = att_gq.shape[1] // 2
    terms[...] = dot(att_gq[:, :half], weights[:, half:], ((1,), (1,))).astype(low)
    grad[...] = dot(att_gq[:, half:], weights[:, :half], ((1,), (1,)))


def back_project(att_gq, weights, step=512):
    tok = att_gq.shape[0]
    width, cols = weights.shape[0], att_gq.shape[1]
    out = pl.BlockSpec((tok, step), lambda i: (0, i))
    return pl.pallas_call(
        back_project_kernel,
        grid=(width // step,),
        in_specs=[
            pl.BlockSpec(att_gq.shape, lambda i: (0, 0)),
            pl.BlockSpec((step, cols), lambda i: (i, 0)),
        ],
        out_specs=[out, out],
        out_shape=[
            jax.ShapeDtypeStruct((tok, width), low),
            jax.ShapeDtypeStruct((tok, width), wide),
        ],
        compiler_params=PARAMS,
    )(att_gq, weights)


def weight_grad_kernel(rows, att_gq, grad_o, grad_q):
    half, block = att_gq.shape[1] // 2, rows.shape[1] // 2

    @pl.when(pl.program_id(0) == 0)
    def _():
        grad_o[...] = jnp.zeros_like(grad_o)
        grad_q[...] = jnp.zeros_like(grad_q)

    grad_o[...] += dot(rows[:, :block], att_gq[:, :half], ((0,), (0,)))
    grad_q[...] += dot(rows[:, block:], att_gq[:, half:], ((0,), (0,)))


def weight_grads(rows, att_gq, step=512):
    seq_len, cols = att_gq.shape
    out = jax.ShapeDtypeStruct((rows.shape[1] // 2, cols // 2), wide)
    return pl.pallas_call(
        weight_grad_kernel,
        grid=(seq_len // step,),
        in_specs=[
            pl.BlockSpec((step, rows.shape[1]), lambda i: (i, 0)),
            pl.BlockSpec((step, cols), lambda i: (i, 0)),
        ],
        out_specs=[pl.BlockSpec(out.shape, lambda i: (0, 0))] * 2,
        out_shape=[out, out],
        compiler_params=PARAMS,
    )(rows, att_gq)


def on_device(
    stream_in, pending, gain, q_weight, k_weight, v_weight, out_weight, grad_out, doc_ids
):
    y, z, c, h, x = (lax.axis_index(a) for a in ("y", "z", "c", "h", "x"))
    tens_index = h * NX + x
    rows_own, width = stream_in.shape
    tok = pending.shape[1]
    outer = SIZES["y"] * SIZES["z"]
    n_dp = outer * 2
    block = width // n_dp
    q_width = q_weight.shape[1]
    seq_len = doc_ids.shape[0]

    kv_first = tens_index * (q_width // HEAD_DIM) // (HEADS // KV_HEADS) * HEAD_DIM
    kv_weights = [
        lax.dynamic_slice_in_dim(w, kv_first, HEAD_DIM, 1) for w in (k_weight, v_weight)
    ]
    weights = lax.all_gather(
        jnp.concatenate([q_weight, out_weight] + kv_weights, axis=1), DP, axis=0, tiled=True
    )

    stream_f = stream_in.astype(wide)
    inv_rms = lax.rsqrt(jnp.mean(stream_f * stream_f, axis=-1, keepdims=True) + eps)
    unit_rows = stream_f * inv_rms
    normed_own = (unit_rows * gain).astype(low)
    both = jnp.concatenate([normed_own, grad_out], axis=1)
    both = spread_tensor(both).reshape(tok, 2 * width)

    def index(axis):
        return lax.broadcasted_iota(jnp.int32, (NX, 2, rows_own), axis)

    local = (((h ^ index(1)) * NX + (x + index(0)) % NX) * rows_own + index(2)).reshape(tok)
    block_first = ((y * SIZES["z"] + z) * 2 + c) * tok
    places = block_first + local
    rel_c = jnp.arange(2, dtype=jnp.int32)[:, None, None]
    at_yz = jnp.arange(outer, dtype=jnp.int32)[None, :, None]
    key_place = ((at_yz * 2 + (c ^ rel_c)) * tok + local[None, None, :]).reshape(seq_len, 1)

    def relative(a):
        a = a.reshape((2, NX, rows_own) + a.shape[1:])
        a = jnp.where(h == 0, a, a[::-1])
        a = lax.dynamic_slice_in_dim(jnp.concatenate([a, a], axis=1), x, NX, 1)
        return jnp.swapaxes(a, 0, 1)

    doc_query = relative(lax.dynamic_slice_in_dim(doc_ids, block_first, tok)).reshape(tok)
    first_place = jnp.sum((doc_ids[None, :] < doc_query[:, None]).astype(jnp.int32), axis=1)

    frequency = rope_base ** (-2.0 * jnp.arange(HALF_DIM).astype(wide) / HEAD_DIM)
    angles = places.astype(wide)[:, None] * frequency[None, :]
    cosine, sine = jnp.cos(angles), jnp.sin(angles)
    cosine = jnp.concatenate([cosine, cosine], axis=1)
    sine = jnp.concatenate([-sine, sine], axis=1)

    def rotate(field, sign):
        flipped = jnp.concatenate([field[:, HALF_DIM:], field[:, :HALF_DIM]], axis=1)
        return field * cosine + sign * flipped * sine

    split = [a.reshape(rows_own, n_dp, block) for a in (grad_out, normed_own)]
    rows = jnp.transpose(jnp.concatenate(split, axis=2), (1, 0, 2))
    rows = spread_tensor(lax.all_to_all(rows, DP, 0, 0, tiled=True))
    rows = jnp.transpose(rows, (2, 0, 1, 3, 4)).reshape(seq_len, 2 * block)
    normed_cores = rows[:, block:].reshape(outer, 2, tok, block)
    rows_near, rows_far = (
        lax.dynamic_index_in_dim(normed_cores, i, 1, keepdims=False).reshape(-1, block)
        for i in (c, 1 - c)
    )
    pend = relative(pending[0])

    kv_own = kv_project(both, weights, cosine, sine, rows, pend)
    kv_near = spread_yz(kv_own)
    kv_far = swap(kv_near, "c")
    query, grad_heads = project(both, weights, cosine, sine, 2 * q_width)
    bounds = jnp.stack([places, first_place])
    att_gq, near_piece, far_piece = attend(
        query, grad_heads, kv_near, kv_far, key_place, bounds, cosine, sine
    )
    kv_sum = near_piece.astype(wide) + swap(far_piece, "c").astype(wide)
    kv_sum = kv_sum.astype(low).reshape(SIZES["y"], -1, 2 * HEAD_DIM)
    kv_sum = collect(kv_sum, "y").astype(low)
    att_gq_all = lax.all_gather(hold(att_gq, kv_sum), DP, axis=0, tiled=True)
    kv_grad = collect(kv_sum.reshape(SIZES["z"], tok, 2 * HEAD_DIM), "z")
    grad_key = rotate(kv_grad[:, :HEAD_DIM], -1.0)
    grad_kv = jnp.concatenate([grad_key, kv_grad[:, HEAD_DIM:]], axis=1).astype(low)

    gkv_near = spread_yz(grad_kv)
    gkv_far = swap(gkv_near, "c")
    grad_w_kv = dot(rows_near, gkv_near, ((0,), (0,))) + dot(rows_far, gkv_far, ((0,), (0,)))

    terms, query_terms = back_project(att_gq, weights)
    terms = terms.reshape(NX, 2, rows_own, width).astype(wide) + pend.astype(wide)
    hidden_out = (stream_f + collect_tensor(terms.astype(low))).astype(low)

    wkv = weights[:, 2 * q_width :]
    normed_terms = query_terms + dot(grad_kv, wkv, ((1,), (1,)))
    grad_normed = collect_tensor(normed_terms.astype(low).reshape(NX, 2, rows_own, width))
    gain_sum = jnp.sum(normed_terms * both[:, :width].astype(wide), axis=0).reshape(n_dp, block)
    for axis in ("c", "h", "x", "y", "z"):
        gain_sum = all_sum(gain_sum, axis)
    grad_gain = gain_sum.reshape(width) / gain

    grad_o, grad_q = weight_grads(rows, att_gq_all)

    kv_own_w = grad_w_kv.astype(low)
    kv_blocks = [kv_own_w.astype(wide)] + [shift(kv_own_w, k).astype(wide) for k in range(1, NX)]
    odd = x % 2 == 1
    near = kv_blocks[0] + jnp.where(odd, kv_blocks[3], kv_blocks[1])
    far = kv_blocks[2] + jnp.where(odd, kv_blocks[1], kv_blocks[3])
    pair = jnp.stack([jnp.where(x < 2, near, far), jnp.where(x < 2, far, near)]).astype(low)
    other = swap(pair, "h")
    pair = jnp.concatenate(
        [jnp.where(h == 0, pair, other), jnp.where(h == 0, other, pair)], axis=0
    ).astype(wide)
    grad_k, grad_v = (
        jnp.transpose(pair[:, :, i : i + HEAD_DIM], (1, 0, 2)).reshape(k_weight.shape)
        for i in (0, HEAD_DIM)
    )

    scaled_grad = grad_normed * gain
    grad_stream = (
        inv_rms
        * (scaled_grad - unit_rows * jnp.mean(scaled_grad * unit_rows, axis=-1, keepdims=True))
        + grad_out.astype(wide)
    ).astype(low)
    return (hidden_out, grad_stream, grad_gain, grad_q, grad_k, grad_v, grad_o)


def solution(mesh):
    fine = Mesh(mesh.devices.reshape(tuple(SIZES.values())), tuple(SIZES))
    whole = P(DP + TENSOR, None)
    in_specs = (
        whole,
        P(TENSOR, DP, None),
        P(),
        P(DP, TENSOR),
        P(DP, None),
        P(DP, None),
        P(DP, TENSOR),
        whole,
        P(),
    )
    out_specs = (whole, whole, P(), P(DP, TENSOR), P(DP, None), P(DP, None), P(DP, TENSOR))
    return jax.shard_map(
        on_device, mesh=fine, in_specs=in_specs, out_specs=out_specs, check_vma=False
    )
```

```python
import jax
import jax.numpy as jnp
from jax import lax
from jax.experimental import pallas as pl
from jax.experimental.pallas import tpu as pltpu
from jax.sharding import Mesh
from jax.sharding import PartitionSpec as P

HEADS = 32
KV_HEADS = 4
HEAD_DIM = 128
HALF_DIM = HEAD_DIM // 2

eps = 1e-05
rope_base = 500000.0

SIZES = {"y": 4, "z": 4, "c": 2, "h": 2, "x": 4}
DP = ("y", "z", "c")
TENSOR = ("h", "x")
NX = SIZES["x"]
wide = jnp.float32
low = jnp.bfloat16


def dot(a, b, dims):
    return lax.dot_general(a, b, (dims, ((), ())), preferred_element_type=wide)


def swap(a, axis):
    return lax.ppermute(a, axis, [(0, 1), (1, 0)])


def shift(a, step):
    return lax.ppermute(a, "x", [((i + step) % NX, i) for i in range(NX)])


def spread(a, axis):
    size = SIZES[axis]
    return lax.all_to_all(
        jnp.broadcast_to(a[None], (size,) + a.shape), axis, 0, 0, tiled=True
    )


def spread_yz(a):
    rows, cols = a.shape
    a = spread(a, "z").reshape(SIZES["z"] * rows, cols)
    return spread(a, "y").reshape(SIZES["y"] * SIZES["z"] * rows, cols)


def collect(a, axis):
    return jnp.sum(lax.all_to_all(a, axis, 0, 0, tiled=True).astype(wide), axis=0)


def all_sum(a, axis):
    if SIZES[axis] == 2:
        return a + swap(a, axis)
    far = [lax.ppermute(a, axis, [(i, i ^ k) for i in range(4)]) for k in range(1, 4)]
    return (a + far[0]) + (far[1] + far[2])


def spread_tensor(a):
    both = jnp.stack([a, swap(a, "h")])
    return jnp.stack([both] + [shift(both, k) for k in range(1, NX)])


def collect_tensor(a):
    total = a[0].astype(wide)
    for k in range(1, NX):
        total = total + shift(a[k], NX - k).astype(wide)
    return total[0] + swap(total[1].astype(low), "h").astype(wide)


def turn(field, cosine, sine):
    return field * cosine + pltpu.roll(field, HALF_DIM, 1) * sine


PARAMS = pltpu.CompilerParams(vmem_limit_bytes=48 * 2**20)
ANY = pl.BlockSpec(memory_space=pl.ANY)


def kv_project_kernel(normed, weights, cosine, sine, kv, total):
    step = pl.program_id(0)

    @pl.when(step == 0)
    def _():
        total[...] = jnp.zeros_like(total)

    total[...] += dot(normed[...], weights[...], ((1,), (0,)))

    @pl.when(step == pl.num_programs(0) - 1)
    def _():
        kv[:, :HEAD_DIM] = turn(total[:, :HEAD_DIM], cosine[...], sine[...]).astype(low)
        kv[:, HEAD_DIM:] = total[:, HEAD_DIM:].astype(low)


def kv_project(normed, weights, cosine, sine, step=1024):
    tok, width = normed.shape
    kv_cols = weights.shape[1]
    fixed = pl.BlockSpec((tok, HEAD_DIM), lambda i: (0, 0))
    return pl.pallas_call(
        kv_project_kernel,
        grid=(width // step,),
        in_specs=[
            pl.BlockSpec((tok, step), lambda i: (0, i)),
            pl.BlockSpec((step, kv_cols), lambda i: (i, 0)),
            fixed,
            fixed,
        ],
        out_specs=pl.BlockSpec((tok, kv_cols), lambda i: (0, 0)),
        out_shape=jax.ShapeDtypeStruct((tok, kv_cols), low),
        scratch_shapes=[pltpu.VMEM((tok, kv_cols), wide)],
        compiler_params=PARAMS,
    )(normed, weights, cosine, sine)


def project_kernel(
    normed, grads, weights, cosine, sine, rows, pend, query, grad_heads, total
):
    step = pl.program_id(0)
    tok, half = normed.shape[0], weights.shape[1] // 2

    @pl.when(step == 0)
    def _():
        total[...] = jnp.zeros_like(total)

    total[:, :half] += dot(normed[...], weights[:, :half], ((1,), (0,)))
    total[:, half:] += dot(grads[...], weights[:, half:], ((1,), (0,)))

    @pl.when(step == pl.num_programs(0) - 1)
    def _():
        for i in range(half // HEAD_DIM):
            at = pl.ds(i * tok, tok)
            query[at, :] = turn(
                total[:, i * HEAD_DIM : (i + 1) * HEAD_DIM], cosine[...], sine[...]
            ).astype(low)
            grad_heads[at, :] = total[
                :, half + i * HEAD_DIM : half + (i + 1) * HEAD_DIM
            ].astype(low)


def project(normed, grads, weights, cosine, sine, rows, pend, step=512):
    tok, width = normed.shape
    cols = weights.shape[1]
    out = jax.ShapeDtypeStruct((cols // 2 // HEAD_DIM * tok, HEAD_DIM), low)
    fixed = pl.BlockSpec((tok, HEAD_DIM), lambda i: (0, 0))
    return pl.pallas_call(
        project_kernel,
        grid=(width // step,),
        in_specs=[
            pl.BlockSpec((tok, step), lambda i: (0, i)),
            pl.BlockSpec((tok, step), lambda i: (0, i)),
            pl.BlockSpec((step, cols), lambda i: (i, 0)),
            fixed,
            fixed,
            ANY,
            ANY,
        ],
        out_specs=[pl.BlockSpec(out.shape, lambda i: (0, 0))] * 2,
        out_shape=[out, out],
        scratch_shapes=[pltpu.VMEM((tok, cols), wide)],
        compiler_params=PARAMS,
    )(normed, grads, weights, cosine, sine, rows, pend)


def hold_kernel(value, other, third, out):
    out[...] = value[...]


def hold(value, other, third):
    return pl.pallas_call(
        hold_kernel,
        in_specs=[pl.BlockSpec(memory_space=pltpu.VMEM), ANY, ANY],
        out_shape=jax.ShapeDtypeStruct(value.shape, value.dtype),
    )(value, other, third)


def attend_kernel(
    query, grad_heads, near, far, key_place, bounds, cosine, sine, att_gq, near_grad, far_grad, score
):
    rows = query.shape[0]
    tok = cosine.shape[0]
    heads = rows // tok
    half = near.shape[0]
    step = 512
    scale = HEAD_DIM ** (-0.5)
    q, g = query[...], grad_heads[...]
    last, first = bounds[0:1, :], bounds[1:2, :]

    peak = jnp.full((1, rows), -1e30, wide)
    for kv, base in ((near, 0), (far, half)):

        def mark(i, peak, kv=kv, base=base):
            at = pl.multiple_of(i * step, step)
            s = dot(kv[pl.ds(at, step), :HEAD_DIM], q, ((1,), (1,))) * scale
            place = key_place[pl.ds(base + at, step), :]
            place = jnp.broadcast_to(place, (step, tok))
            bias = jnp.where((place <= last) & (place >= first), 0.0, -1e30)
            s = s + jnp.concatenate([bias] * heads, axis=1)
            score[pl.ds(base + at, step), :] = s
            return jnp.maximum(peak, jnp.max(s, axis=0, keepdims=True))

        peak = lax.fori_loop(0, half // step, mark, peak)

    carry = (jnp.zeros((1, rows), wide), jnp.zeros((HEAD_DIM, rows), wide))
    for kv, base in ((near, 0), (far, half)):

        def weigh(i, carry, kv=kv, base=base):
            norm, out = carry
            at = pl.multiple_of(i * step, step)
            e = jnp.exp(score[pl.ds(base + at, step), :] - peak)
            score[pl.ds(base + at, step), :] = e
            out = out + dot(kv[pl.ds(at, step), HEAD_DIM:], e.astype(low), ((0,), (0,)))
            return norm + jnp.sum(e, axis=0, keepdims=True), out

        carry = lax.fori_loop(0, half // step, weigh, carry)
    norm, out = carry
    inverse = 1.0 / norm
    out = (out * inverse).astype(low).astype(wide)
    delta = jnp.sum(out * g.astype(wide).T, axis=0, keepdims=True)

    grad_query = jnp.zeros((HEAD_DIM, rows), wide)
    for kv, grad, base in ((near, near_grad, 0), (far, far_grad, half)):

        def back(i, grad_query, kv=kv, grad=grad, base=base):
            at = pl.multiple_of(i * step, step)
            p = score[pl.ds(base + at, step), :] * inverse
            gp = dot(kv[pl.ds(at, step), HEAD_DIM:], g, ((1,), (1,)))
            gs = (p * (gp - delta)).astype(low)
            grad[pl.ds(at, step), :HEAD_DIM] = (dot(gs, q, ((1,), (0,))) * scale).astype(low)
            grad[pl.ds(at, step), HEAD_DIM:] = dot(p.astype(low), g, ((1,), (0,))).astype(low)
            return grad_query + dot(kv[pl.ds(at, step), :HEAD_DIM], gs, ((0,), (0,)))

        grad_query = lax.fori_loop(0, half // step, back, grad_query)

    for i in range(heads):
        at, cols = slice(i * tok, (i + 1) * tok), slice(i * HEAD_DIM, (i + 1) * HEAD_DIM)
        att_gq[:, cols] = out[:, at].T.astype(low)
        back_cols = slice(heads * HEAD_DIM + cols.start, heads * HEAD_DIM + cols.stop)
        att_gq[:, back_cols] = turn(
            grad_query[:, at].T * scale, cosine[...], -sine[...]
        ).astype(low)


def attend(query, grad_heads, near, far, key_place, bounds, cosine, sine):
    rows, tok = query.shape[0], cosine.shape[0]
    half = near.shape[0]
    return pl.pallas_call(
        attend_kernel,
        out_shape=[
            jax.ShapeDtypeStruct((tok, 2 * rows // tok * HEAD_DIM), low),
            jax.ShapeDtypeStruct(near.shape, low),
            jax.ShapeDtypeStruct(far.shape, low),
        ],
        scratch_shapes=[pltpu.VMEM((2 * half, rows), wide)],
        compiler_params=PARAMS,
    )(query, grad_heads, near, far, key_place, bounds, cosine, sine)


def back_project_kernel(att_gq, weights, rows, terms, grad):
    half = att_gq.shape[1] // 2
    terms[...] = dot(att_gq[:, :half], weights[:, half:], ((1,), (1,))).astype(low)
    grad[...] = dot(att_gq[:, half:], weights[:, :half], ((1,), (1,)))


def back_project(att_gq, weights, rows, step=512):
    tok = att_gq.shape[0]
    width, cols = weights.shape[0], att_gq.shape[1]
    out = pl.BlockSpec((tok, step), lambda i: (0, i))
    return pl.pallas_call(
        back_project_kernel,
        grid=(width // step,),
        in_specs=[
            pl.BlockSpec(att_gq.shape, lambda i: (0, 0)),
            pl.BlockSpec((step, cols), lambda i: (i, 0)),
            ANY,
        ],
        out_specs=[out, out],
        out_shape=[
            jax.ShapeDtypeStruct((tok, width), low),
            jax.ShapeDtypeStruct((tok, width), wide),
        ],
        compiler_params=PARAMS,
    )(att_gq, weights, rows)


def weight_grad_kernel(rows, att_gq, grad_o, grad_q):
    half, block = att_gq.shape[1] // 2, rows.shape[1] // 2

    @pl.when(pl.program_id(0) == 0)
    def _():
        grad_o[...] = jnp.zeros_like(grad_o)
        grad_q[...] = jnp.zeros_like(grad_q)

    grad_o[...] += dot(rows[:, :block], att_gq[:, :half], ((0,), (0,)))
    grad_q[...] += dot(rows[:, block:], att_gq[:, half:], ((0,), (0,)))


def weight_grads(rows, att_gq, step=512):
    seq_len, cols = att_gq.shape
    out = jax.ShapeDtypeStruct((rows.shape[1] // 2, cols // 2), wide)
    return pl.pallas_call(
        weight_grad_kernel,
        grid=(seq_len // step,),
        in_specs=[
            pl.BlockSpec((step, rows.shape[1]), lambda i: (i, 0)),
            pl.BlockSpec((step, cols), lambda i: (i, 0)),
        ],
        out_specs=[pl.BlockSpec(out.shape, lambda i: (0, 0))] * 2,
        out_shape=[out, out],
        compiler_params=PARAMS,
    )(rows, att_gq)


def kv_weight_grad_kernel(core, rows, near, far, waited, out):
    block = rows.shape[3] // 2

    @pl.when(pl.program_id(0) == 0)
    def _():
        out[...] = jnp.zeros_like(out)

    c = core[0]
    for i in range(rows.shape[0]):
        out[...] += dot(rows[i, c][:, block:], near[i], ((0,), (0,)))
        out[...] += dot(rows[i, 1 - c][:, block:], far[i], ((0,), (0,)))


def kv_weight_grad(core, rows, near, far, waited, step=4):
    outer, cores, tok, both = rows.shape
    kv = pl.BlockSpec((step,) + near.shape[1:], lambda i, c: (i, 0, 0))
    return pl.pallas_call(
        kv_weight_grad_kernel,
        grid_spec=pltpu.PrefetchScalarGridSpec(
            num_scalar_prefetch=1,
            grid=(outer // step,),
            in_specs=[
                pl.BlockSpec((step, cores, tok, both), lambda i, c: (i, 0, 0, 0)),
                kv,
                kv,
                ANY,
            ],
            out_specs=pl.BlockSpec((both // 2, near.shape[2]), lambda i, c: (0, 0)),
        ),
        out_shape=jax.ShapeDtypeStruct((both // 2, near.shape[2]), wide),
        compiler_params=PARAMS,
    )(core, rows, near, far, waited)


def on_device(
    stream_in, pending, gain, q_weight, k_weight, v_weight, out_weight, grad_out, doc_ids
):
    y, z, c, h, x = (lax.axis_index(a) for a in ("y", "z", "c", "h", "x"))
    tens_index = h * NX + x
    rows_own, width = stream_in.shape
    tok = pending.shape[1]
    outer = SIZES["y"] * SIZES["z"]
    n_dp = outer * 2
    block = width // n_dp
    q_width = q_weight.shape[1]
    seq_len = doc_ids.shape[0]

    def by_core(near):
        cols = near.shape[1]
        far = swap(near, "c")
        near, far = (a.reshape(outer, 1, near.shape[0] // outer, cols) for a in (near, far))
        pair = [jnp.where(c == 0, near, far), jnp.where(c == 0, far, near)]
        return jnp.concatenate(pair, axis=1).reshape(-1, cols)

    kv_first = tens_index * (q_width // HEAD_DIM) // (HEADS // KV_HEADS) * HEAD_DIM
    kv_weights = [
        lax.dynamic_slice_in_dim(w, kv_first, HEAD_DIM, 1) for w in (k_weight, v_weight)
    ]
    wkv = by_core(spread_yz(jnp.concatenate(kv_weights, axis=1)))
    weights = lax.all_gather(
        jnp.concatenate([q_weight, out_weight], axis=1), DP, axis=0, tiled=True
    )

    stream_f = stream_in.astype(wide)
    inv_rms = lax.rsqrt(jnp.mean(stream_f * stream_f, axis=-1, keepdims=True) + eps)
    unit_rows = stream_f * inv_rms
    normed_own = (unit_rows * gain).astype(low)
    normed = spread_tensor(normed_own).reshape(tok, width)
    grads = spread_tensor(grad_out).reshape(tok, width)

    def index(axis):
        return lax.broadcasted_iota(jnp.int32, (NX, 2, rows_own), axis)

    local = (((h ^ index(1)) * NX + (x + index(0)) % NX) * rows_own + index(2)).reshape(tok)
    block_first = ((y * SIZES["z"] + z) * 2 + c) * tok
    places = block_first + local
    rel_c = jnp.arange(2, dtype=jnp.int32)[:, None, None]
    at_yz = jnp.arange(outer, dtype=jnp.int32)[None, :, None]
    key_place = ((at_yz * 2 + (c ^ rel_c)) * tok + local[None, None, :]).reshape(seq_len, 1)

    def relative(a):
        a = a.reshape((2, NX, rows_own) + a.shape[1:])
        a = jnp.where(h == 0, a, a[::-1])
        a = lax.dynamic_slice_in_dim(jnp.concatenate([a, a], axis=1), x, NX, 1)
        return jnp.swapaxes(a, 0, 1)

    doc_query = relative(lax.dynamic_slice_in_dim(doc_ids, block_first, tok)).reshape(tok)
    first_place = jnp.sum((doc_ids[None, :] < doc_query[:, None]).astype(jnp.int32), axis=1)

    frequency = rope_base ** (-2.0 * jnp.arange(HALF_DIM).astype(wide) / HEAD_DIM)
    angles = places.astype(wide)[:, None] * frequency[None, :]
    cosine, sine = jnp.cos(angles), jnp.sin(angles)
    cosine = jnp.concatenate([cosine, cosine], axis=1)
    sine = jnp.concatenate([-sine, sine], axis=1)

    def rotate(field, sign):
        flipped = jnp.concatenate([field[:, HALF_DIM:], field[:, :HALF_DIM]], axis=1)
        return field * cosine + sign * flipped * sine

    kv_own = kv_project(normed, wkv, cosine, sine)
    kv_near = spread_yz(kv_own)
    kv_far = swap(kv_near, "c")

    split = [a.reshape(rows_own, n_dp, block) for a in (grad_out, normed_own)]
    rows = jnp.transpose(jnp.concatenate(split, axis=2), (1, 0, 2))
    rows = lax.all_to_all(hold(rows, kv_near, kv_near), DP, 0, 0, tiled=True)
    pend = relative(pending[0])

    query, grad_heads = project(normed, grads, weights, cosine, sine, rows, pend)
    rows = jnp.transpose(spread_tensor(rows), (2, 0, 1, 3, 4)).reshape(seq_len, 2 * block)
    bounds = jnp.stack([places, first_place])
    att_gq, near_piece, far_piece = attend(
        query, grad_heads, kv_near, kv_far, key_place, bounds, cosine, sine
    )
    kv_sum = near_piece.astype(wide) + swap(far_piece, "c").astype(wide)
    kv_sum = kv_sum.astype(low).reshape(SIZES["y"], -1, 2 * HEAD_DIM)
    kv_sum = collect(kv_sum, "y").astype(low)
    terms, query_terms = back_project(att_gq, weights, rows)
    att_gq_all = lax.all_gather(hold(att_gq, kv_sum, terms), DP, axis=0, tiled=True)
    grad_o, grad_q = weight_grads(rows, att_gq_all)
    kv_grad = collect(kv_sum.reshape(SIZES["z"], tok, 2 * HEAD_DIM), "z")
    grad_key = rotate(kv_grad[:, :HEAD_DIM], -1.0)
    grad_kv = jnp.concatenate([grad_key, kv_grad[:, HEAD_DIM:]], axis=1).astype(low)

    gkv_near = spread_yz(grad_kv)
    gkv_far = swap(gkv_near, "c")
    grad_w_kv = kv_weight_grad(
        c.astype(jnp.int32)[None],
        rows.reshape(outer, 2, tok, 2 * block),
        gkv_near.reshape(outer, tok, 2 * HEAD_DIM),
        gkv_far.reshape(outer, tok, 2 * HEAD_DIM),
        grad_o,
    )

    terms = terms.reshape(NX, 2, rows_own, width).astype(wide) + pend.astype(wide)
    hidden_out = (stream_f + collect_tensor(terms.astype(low))).astype(low)

    normed_terms = query_terms + dot(grad_kv, wkv, ((1,), (1,)))
    grad_normed = collect_tensor(normed_terms.astype(low).reshape(NX, 2, rows_own, width))
    gain_sum = jnp.sum(normed_terms * normed.astype(wide), axis=0).reshape(n_dp, block)
    for axis in ("c", "h", "x", "y", "z"):
        gain_sum = all_sum(gain_sum, axis)
    grad_gain = gain_sum.reshape(width) / gain

    kv_own_w = grad_w_kv.astype(low)
    kv_blocks = [kv_own_w.astype(wide)] + [shift(kv_own_w, k).astype(wide) for k in range(1, NX)]
    odd = x % 2 == 1
    near = kv_blocks[0] + jnp.where(odd, kv_blocks[3], kv_blocks[1])
    far = kv_blocks[2] + jnp.where(odd, kv_blocks[1], kv_blocks[3])
    pair = jnp.stack([jnp.where(x < 2, near, far), jnp.where(x < 2, far, near)]).astype(low)
    other = swap(pair, "h")
    pair = jnp.concatenate(
        [jnp.where(h == 0, pair, other), jnp.where(h == 0, other, pair)], axis=0
    ).astype(wide)
    grad_k, grad_v = (
        jnp.transpose(pair[:, :, i : i + HEAD_DIM], (1, 0, 2)).reshape(k_weight.shape)
        for i in (0, HEAD_DIM)
    )

    scaled_grad = grad_normed * gain
    grad_stream = (
        inv_rms
        * (scaled_grad - unit_rows * jnp.mean(scaled_grad * unit_rows, axis=-1, keepdims=True))
        + grad_out.astype(wide)
    ).astype(low)
    return (hidden_out, grad_stream, grad_gain, grad_q, grad_k, grad_v, grad_o)


def solution(mesh):
    fine = Mesh(mesh.devices.reshape(tuple(SIZES.values())), tuple(SIZES))
    whole = P(DP + TENSOR, None)
    in_specs = (
        whole,
        P(TENSOR, DP, None),
        P(),
        P(DP, TENSOR),
        P(DP, None),
        P(DP, None),
        P(DP, TENSOR),
        whole,
        P(),
    )
    out_specs = (whole, whole, P(), P(DP, TENSOR), P(DP, None), P(DP, None), P(DP, TENSOR))
    return jax.shard_map(
        on_device, mesh=fine, in_specs=in_specs, out_specs=out_specs, check_vma=False
    )
```

```python
import jax
import jax.numpy as jnp
from jax import lax
from jax.experimental import pallas as pl
from jax.experimental.pallas import tpu as pltpu
from jax.sharding import Mesh
from jax.sharding import PartitionSpec as P

HEADS = 32
KV_HEADS = 4
HEAD_DIM = 128
HALF_DIM = HEAD_DIM // 2

eps = 1e-05
rope_base = 500000.0

SIZES = {"y": 4, "z": 4, "c": 2, "h": 2, "x": 4}
DP = ("y", "z", "c")
TENSOR = ("h", "x")
NX = SIZES["x"]
wide = jnp.float32
low = jnp.bfloat16


def dot(a, b, dims):
    return lax.dot_general(a, b, (dims, ((), ())), preferred_element_type=wide)


def swap(a, axis):
    return lax.ppermute(a, axis, [(0, 1), (1, 0)])


def shift(a, step):
    return lax.ppermute(a, "x", [((i + step) % NX, i) for i in range(NX)])


def spread(a, axis):
    size = SIZES[axis]
    return lax.all_to_all(
        jnp.broadcast_to(a[None], (size,) + a.shape), axis, 0, 0, tiled=True
    )


def collect(a, axis):
    return jnp.sum(lax.all_to_all(a, axis, 0, 0, tiled=True).astype(wide), axis=0)


def spread_h(a):
    return jnp.stack([a, swap(a, "h")])


def spread_x(a):
    return [a] + [shift(a, k) for k in range(1, NX)]


def sum_pair(a):
    return a[0].astype(wide) + a[1].astype(wide)


def collect_x(a):
    total = a[0].astype(wide)
    for k in range(1, NX):
        total = total + shift(a[k], NX - k).astype(wide)
    return total[0], total[1].astype(low)


def turn(field, cosine, sine):
    return field * cosine + pltpu.roll(field, HALF_DIM, 1) * sine


ANY = pl.BlockSpec(memory_space=pl.ANY)
PARAMS = pltpu.CompilerParams(vmem_limit_bytes=48 * 2**20)


def kv_project_kernel(normed, weights, cosine, sine, kv, total):
    step = pl.program_id(0)

    @pl.when(step == 0)
    def _():
        total[...] = jnp.zeros_like(total)

    total[...] += dot(normed[...], weights[...], ((1,), (0,)))

    @pl.when(step == pl.num_programs(0) - 1)
    def _():
        kv[:, :HEAD_DIM] = turn(total[:, :HEAD_DIM], cosine[...], sine[...]).astype(low)
        kv[:, HEAD_DIM:] = total[:, HEAD_DIM:].astype(low)


def kv_project(both, weights, cosine, sine, step=1024):
    tok = both.shape[0]
    width, cols = weights.shape
    kv_cols = 2 * HEAD_DIM
    fixed = pl.BlockSpec((tok, HEAD_DIM), lambda i: (0, 0))
    return pl.pallas_call(
        kv_project_kernel,
        grid=(width // step,),
        in_specs=[
            pl.BlockSpec((tok, step), lambda i: (0, i)),
            pl.BlockSpec((step, kv_cols), lambda i: (i, cols // kv_cols - 1)),
            fixed,
            fixed,
        ],
        out_specs=pl.BlockSpec((tok, kv_cols), lambda i: (0, 0)),
        out_shape=jax.ShapeDtypeStruct((tok, kv_cols), low),
        scratch_shapes=[pltpu.VMEM((tok, kv_cols), wide)],
        compiler_params=PARAMS,
    )(both, weights, cosine, sine)


def project_kernel(normed, grads, weights, cosine, sine, query, grad_heads, total):
    step = pl.program_id(0)
    tok, half = normed.shape[0], weights.shape[1] // 2

    @pl.when(step == 0)
    def _():
        total[...] = jnp.zeros_like(total)

    total[:, :half] += dot(normed[...], weights[:, :half], ((1,), (0,)))
    total[:, half:] += dot(grads[...], weights[:, half:], ((1,), (0,)))

    @pl.when(step == pl.num_programs(0) - 1)
    def _():
        for i in range(half // HEAD_DIM):
            at = pl.ds(i * tok, tok)
            query[at, :] = turn(
                total[:, i * HEAD_DIM : (i + 1) * HEAD_DIM], cosine[...], sine[...]
            ).astype(low)
            grad_heads[at, :] = total[
                :, half + i * HEAD_DIM : half + (i + 1) * HEAD_DIM
            ].astype(low)


def project(both, weights, cosine, sine, cols, step=1024):
    tok = both.shape[0]
    width = weights.shape[0]
    steps = width // step
    out = jax.ShapeDtypeStruct((cols // 2 // HEAD_DIM * tok, HEAD_DIM), low)
    fixed = pl.BlockSpec((tok, HEAD_DIM), lambda i: (0, 0))
    return pl.pallas_call(
        project_kernel,
        grid=(steps,),
        in_specs=[
            pl.BlockSpec((tok, step), lambda i: (0, i)),
            pl.BlockSpec((tok, step), lambda i: (0, i + steps)),
            pl.BlockSpec((step, cols), lambda i: (i, 0)),
            fixed,
            fixed,
        ],
        out_specs=[pl.BlockSpec(out.shape, lambda i: (0, 0))] * 2,
        out_shape=[out, out],
        scratch_shapes=[pltpu.VMEM((tok, cols), wide)],
        compiler_params=PARAMS,
    )(both, both, weights, cosine, sine)


def attend_kernel(
    at_chx,
    query,
    grad_heads,
    near,
    far,
    bounds,
    cosine,
    sine,
    att_gq,
    near_grad,
    far_grad,
    score,
):
    rows = query.shape[0]
    tok = cosine.shape[0]
    heads = rows // tok
    half = near.shape[0]
    step = 512
    scale = HEAD_DIM ** (-0.5)
    q, g = query[...], grad_heads[...]
    last, first = bounds[0:1, :], bounds[1:2, :]

    c, h, x = at_chx[0], at_chx[1], at_chx[2]
    key = lax.broadcasted_iota(jnp.int32, (step, tok), 0)
    key_x = (x + (key // 32) % NX) % NX
    key_h = (h + (key // 16) % 2) % 2
    local = (key // tok) * (2 * tok) + (key_h * NX + key_x) * 16 + key % 16

    peak = jnp.full((1, rows), -1e30, wide)
    for kv, base, core in ((near, 0, c), (far, half, 1 - c)):

        def mark(i, peak, kv=kv, base=base, core=core):
            at = pl.multiple_of(i * step, step)
            s = dot(kv[pl.ds(at, step), :HEAD_DIM], q, ((1,), (1,))) * scale
            place = local + (2 * at + core * tok)
            bias = jnp.where((place <= last) & (place >= first), 0.0, -1e30)
            s = s + jnp.concatenate([bias] * heads, axis=1)
            score[pl.ds(base + at, step), :] = s
            return jnp.maximum(peak, jnp.max(s, axis=0, keepdims=True))

        peak = lax.fori_loop(0, half // step, mark, peak)

    carry = (jnp.zeros((1, rows), wide), jnp.zeros((HEAD_DIM, rows), wide))
    for kv, base in ((near, 0), (far, half)):

        def weigh(i, carry, kv=kv, base=base):
            norm, out = carry
            at = pl.multiple_of(i * step, step)
            e = jnp.exp(score[pl.ds(base + at, step), :] - peak)
            score[pl.ds(base + at, step), :] = e
            out = out + dot(kv[pl.ds(at, step), HEAD_DIM:], e.astype(low), ((0,), (0,)))
            return norm + jnp.sum(e, axis=0, keepdims=True), out

        carry = lax.fori_loop(0, half // step, weigh, carry)
    norm, out = carry
    inverse = 1.0 / norm
    out = (out * inverse).astype(low).astype(wide)
    delta = jnp.sum(out * g.astype(wide).T, axis=0, keepdims=True)

    grad_query = jnp.zeros((HEAD_DIM, rows), wide)
    for kv, grad, base in ((near, near_grad, 0), (far, far_grad, half)):

        def back(i, grad_query, kv=kv, grad=grad, base=base):
            at = pl.multiple_of(i * step, step)
            p = score[pl.ds(base + at, step), :] * inverse
            gp = dot(kv[pl.ds(at, step), HEAD_DIM:], g, ((1,), (1,)))
            gs = (p * (gp - delta)).astype(low)
            grad[pl.ds(at, step), :HEAD_DIM] = (dot(gs, q, ((1,), (0,))) * scale).astype(low)
            grad[pl.ds(at, step), HEAD_DIM:] = dot(p.astype(low), g, ((1,), (0,))).astype(low)
            return grad_query + dot(kv[pl.ds(at, step), :HEAD_DIM], gs, ((0,), (0,)))

        grad_query = lax.fori_loop(0, half // step, back, grad_query)

    for i in range(heads):
        at, cols = slice(i * tok, (i + 1) * tok), slice(i * HEAD_DIM, (i + 1) * HEAD_DIM)
        att_gq[:, cols] = out[:, at].T.astype(low)
        back_cols = slice(heads * HEAD_DIM + cols.start, heads * HEAD_DIM + cols.stop)
        att_gq[:, back_cols] = turn(
            grad_query[:, at].T * scale, cosine[...], -sine[...]
        ).astype(low)


def attend(at_chx, query, grad_heads, near, far, bounds, cosine, sine):
    rows, tok = query.shape[0], cosine.shape[0]
    half = near.shape[0]
    vmem = pl.BlockSpec(memory_space=pltpu.VMEM)
    return pl.pallas_call(
        attend_kernel,
        in_specs=[pl.BlockSpec(memory_space=pltpu.SMEM)] + [vmem] * 7,
        out_shape=[
            jax.ShapeDtypeStruct((tok, 2 * rows // tok * HEAD_DIM), low),
            jax.ShapeDtypeStruct(near.shape, low),
            jax.ShapeDtypeStruct(far.shape, low),
        ],
        scratch_shapes=[pltpu.VMEM((2 * half, rows), wide)],
        compiler_params=PARAMS,
    )(at_chx, query, grad_heads, near, far, bounds, cosine, sine)


def back_project_kernel(att_gq, weights, waited, terms, grad):
    half = att_gq.shape[1] // 2
    terms[...] = dot(att_gq[:, :half], weights[:, half:], ((1,), (1,))).astype(low)
    grad[...] = dot(att_gq[:, half:], weights[:, :half], ((1,), (1,)))


def back_project(att_gq, weights, waited, step=1024):
    tok = att_gq.shape[0]
    width, cols = weights.shape[0], att_gq.shape[1]
    out = pl.BlockSpec((tok, step), lambda i: (0, i))
    return pl.pallas_call(
        back_project_kernel,
        grid=(width // step,),
        in_specs=[
            pl.BlockSpec(att_gq.shape, lambda i: (0, 0)),
            pl.BlockSpec((step, cols), lambda i: (i, 0)),
            ANY,
        ],
        out_specs=[out, out],
        out_shape=[
            jax.ShapeDtypeStruct((tok, width), low),
            jax.ShapeDtypeStruct((tok, width), wide),
        ],
        compiler_params=PARAMS,
    )(att_gq, weights, waited)


def normed_grad_kernel(query_terms, grad_kv, weights, normed, terms, gain):
    total = query_terms[...] + dot(grad_kv[...], weights[...], ((1,), (1,)))
    terms[...] = total.astype(low)
    gain[...] = jnp.sum(total * normed[...].astype(wide), axis=0, keepdims=True)


def normed_grad(query_terms, grad_kv, weights, both, step=1024):
    tok, width = query_terms.shape
    kv_cols = grad_kv.shape[1]
    at = weights.shape[1] // kv_cols - 1
    columns = pl.BlockSpec((tok, step), lambda i: (0, i))
    return pl.pallas_call(
        normed_grad_kernel,
        grid=(width // step,),
        in_specs=[
            columns,
            pl.BlockSpec((tok, kv_cols), lambda i: (0, 0)),
            pl.BlockSpec((step, kv_cols), lambda i: (i, at)),
            columns,
        ],
        out_specs=[columns, pl.BlockSpec((1, step), lambda i: (0, i))],
        out_shape=[
            jax.ShapeDtypeStruct((tok, width), low),
            jax.ShapeDtypeStruct((1, width), wide),
        ],
        compiler_params=PARAMS,
    )(query_terms, grad_kv, weights, both)


def positions(rows, at):
    return jnp.concatenate([part[j, at] for part in rows for j in range(2)], axis=0)


def weight_grad_kernel(*refs):
    rows, att_gq, grad_o, grad_q = refs[:NX], refs[NX], refs[-2], refs[-1]
    half, block = att_gq.shape[1] // 2, rows[0].shape[3] // 2

    @pl.when(pl.program_id(0) == 0)
    def _():
        grad_o[...] = jnp.zeros_like(grad_o)
        grad_q[...] = jnp.zeros_like(grad_q)

    own = jnp.concatenate([positions(rows, i) for i in range(rows[0].shape[1])], axis=0)
    grad_o[...] += dot(own[:, :block], att_gq[:, :half], ((0,), (0,)))
    grad_q[...] += dot(own[:, block:], att_gq[:, half:], ((0,), (0,)))


def weight_grads(rows, att_gq, step=8):
    two, n_dp, rows_own, both = rows[0].shape
    seq_len, cols = att_gq.shape
    out = jax.ShapeDtypeStruct((both // 2, cols // 2), wide)
    part = pl.BlockSpec((two, step, rows_own, both), lambda i: (0, i, 0, 0))
    return pl.pallas_call(
        weight_grad_kernel,
        grid=(n_dp // step,),
        in_specs=[part] * NX
        + [pl.BlockSpec((seq_len // n_dp * step, cols), lambda i: (i, 0))],
        out_specs=[pl.BlockSpec(out.shape, lambda i: (0, 0))] * 2,
        out_shape=[out, out],
        compiler_params=PARAMS,
    )(*rows, att_gq)


def kv_weight_grad_kernel(core, *refs):
    rows, (near, far, out, total, gains) = refs[:NX], refs[NX:]
    block = rows[0].shape[3] // 2
    tok = near.shape[1] - gains.shape[1]
    step = pl.program_id(0)

    @pl.when(step == 0)
    def _():
        total[...] = jnp.zeros_like(total)
        gains[...] = jnp.zeros_like(gains)

    c = core[0]
    for i in range(near.shape[0]):
        for at, (grad, of) in enumerate(((near, c), (far, 1 - c))):
            own = positions(rows, 2 * i + of)[:, block:]
            total[...] += dot(own, grad[i, :tok], ((0,), (0,)))
            gains[at] += grad[i, tok:].astype(wide)

    @pl.when(step == pl.num_programs(0) - 1)
    def _():
        out[: total.shape[0]] = total[...].astype(low)
        out[total.shape[0] :] = (gains[0] + gains[1]).astype(low)


def kv_weight_grad(core, rows, near, far, tok, step=4):
    two, n_dp, rows_own, both = rows[0].shape
    outer, depth, cols = near.shape
    kv = pl.BlockSpec((step, depth, cols), lambda i, c: (i, 0, 0))
    part = pl.BlockSpec((two, 2 * step, rows_own, both), lambda i, c: (0, i, 0, 0))
    out = jax.ShapeDtypeStruct((both // 2 + depth - tok, cols), low)
    return pl.pallas_call(
        kv_weight_grad_kernel,
        grid_spec=pltpu.PrefetchScalarGridSpec(
            num_scalar_prefetch=1,
            grid=(outer // step,),
            in_specs=[part] * NX + [kv, kv],
            out_specs=pl.BlockSpec(out.shape, lambda i, c: (0, 0)),
            scratch_shapes=[
                pltpu.VMEM((both // 2, cols), wide),
                pltpu.VMEM((2, depth - tok, cols), wide),
            ],
        ),
        out_shape=out,
        compiler_params=PARAMS,
    )(core, *rows, near, far)


def hold_kernel(first, second, waited, first_out, second_out):
    first_out[...] = first[...]
    second_out[...] = second[...]


def hold(first, second, waited):
    vmem = pl.BlockSpec(memory_space=pltpu.VMEM)
    return pl.pallas_call(
        hold_kernel,
        in_specs=[vmem, vmem, ANY],
        out_shape=[jax.ShapeDtypeStruct(a.shape, a.dtype) for a in (first, second)],
        compiler_params=PARAMS,
    )(first, second, waited)


def add_kernel(near, far, rows, out, rows_out):
    out[...] = (near[...].astype(wide) + far[...].astype(wide)).astype(low)
    rows_out[...] = rows[...]


def add(near, far, rows):
    vmem = pl.BlockSpec(memory_space=pltpu.VMEM)
    return pl.pallas_call(
        add_kernel,
        in_specs=[vmem, vmem, vmem],
        out_shape=[jax.ShapeDtypeStruct(a.shape, low) for a in (near, rows)],
        compiler_params=PARAMS,
    )(near, far, rows)


def pair_kernel(sums, waited, out):
    for i in range(2):
        out[i] = (sums[2 * i].astype(wide) + sums[2 * i + 1].astype(wide)).astype(low)


def pairs(sums, waited):
    return pl.pallas_call(
        pair_kernel,
        in_specs=[pl.BlockSpec(memory_space=pltpu.VMEM), ANY],
        out_shape=jax.ShapeDtypeStruct((NX // 2,) + sums.shape[1:], low),
        compiler_params=PARAMS,
    )(sums, waited)


def on_device(
    stream_in, pending, gain, q_weight, k_weight, v_weight, out_weight, grad_out, doc_ids
):
    y, z, c, h, x = (lax.axis_index(a) for a in ("y", "z", "c", "h", "x"))
    tens_index = h * NX + x
    rows_own, width = stream_in.shape
    tok = pending.shape[1]
    outer = SIZES["y"] * SIZES["z"]
    n_dp = outer * 2
    block = width // n_dp
    q_width = q_weight.shape[1]
    seq_len = doc_ids.shape[0]

    kv_first = tens_index * (q_width // HEAD_DIM) // (HEADS // KV_HEADS) * HEAD_DIM
    kv_weights = [
        lax.dynamic_slice_in_dim(w, kv_first, HEAD_DIM, 1) for w in (k_weight, v_weight)
    ]
    weights = lax.all_gather(
        jnp.concatenate([q_weight, out_weight] + kv_weights, axis=1), DP, axis=0, tiled=True
    )

    stream_f = stream_in.astype(wide)
    inv_rms = lax.rsqrt(jnp.mean(stream_f * stream_f, axis=-1, keepdims=True) + eps)
    unit_rows = stream_f * inv_rms
    normed_own = (unit_rows * gain).astype(low)
    both = spread_h(jnp.concatenate([normed_own, grad_out], axis=1))
    both = jnp.stack(spread_x(both)).reshape(tok, 2 * width)

    split = [a.reshape(rows_own, n_dp, block) for a in (grad_out, normed_own)]
    rows = jnp.transpose(jnp.concatenate(split, axis=2), (1, 0, 2))
    rows = lax.all_to_all(rows, DP, 0, 0, tiled=True)

    def index(axis):
        return lax.broadcasted_iota(jnp.int32, (NX, 2, rows_own), axis)

    local = (((h ^ index(1)) * NX + (x + index(0)) % NX) * rows_own + index(2)).reshape(tok)
    block_first = ((y * SIZES["z"] + z) * 2 + c) * tok
    places = block_first + local
    def relative(a):
        a = a.reshape((2, NX, rows_own) + a.shape[1:])
        a = jnp.where(h == 0, a, a[::-1])
        a = lax.dynamic_slice_in_dim(jnp.concatenate([a, a], axis=1), x, NX, 1)
        return jnp.swapaxes(a, 0, 1)

    doc_query = relative(lax.dynamic_slice_in_dim(doc_ids, block_first, tok)).reshape(tok)
    first_place = jnp.sum((doc_ids[None, :] < doc_query[:, None]).astype(jnp.int32), axis=1)

    frequency = rope_base ** (-2.0 * jnp.arange(HALF_DIM).astype(wide) / HEAD_DIM)
    angles = places.astype(wide)[:, None] * frequency[None, :]
    cosine, sine = jnp.cos(angles), jnp.sin(angles)
    cosine = jnp.concatenate([cosine, cosine], axis=1)
    sine = jnp.concatenate([-sine, sine], axis=1)

    def rotate(field, sign):
        flipped = jnp.concatenate([field[:, HALF_DIM:], field[:, :HALF_DIM]], axis=1)
        return field * cosine + sign * flipped * sine

    pend = relative(pending[0])
    bounds = jnp.stack([places, first_place])
    both, rows, pend, bounds, cosine, sine = lax.optimization_barrier(
        (both, rows, pend, bounds, cosine, sine)
    )
    kv_own = kv_project(both, weights, cosine, sine)
    kv_near = spread(kv_own, "z").reshape(-1, 2 * HEAD_DIM)
    query, grad_heads = project(both, weights, cosine, sine, 2 * q_width)
    kv_near = spread(kv_near, "y").reshape(-1, 2 * HEAD_DIM)
    kv_far = swap(kv_near, "c")
    at_chx = jnp.stack([c, h, x]).astype(jnp.int32)
    att_gq, near_piece, far_piece = attend(
        at_chx, query, grad_heads, kv_near, kv_far, bounds, cosine, sine
    )
    kv_sum, rows = add(near_piece, swap(far_piece, "c"), rows)
    kv_sum = kv_sum.reshape(SIZES["y"], -1, 2 * HEAD_DIM)
    rows = spread_h(rows)
    terms, query_terms = back_project(att_gq, weights, rows)
    kv_sum = collect(kv_sum, "y").astype(low)
    att_gq_all = lax.all_gather(att_gq, DP, axis=0, tiled=True)
    kv_grad = collect(kv_sum.reshape(SIZES["z"], tok, 2 * HEAD_DIM), "z")
    grad_key = rotate(kv_grad[:, :HEAD_DIM], -1.0)
    grad_kv = jnp.concatenate([grad_key, kv_grad[:, HEAD_DIM:]], axis=1).astype(low)

    terms = terms.reshape(NX, 2, rows_own, width).astype(wide) + pend.astype(wide)
    hidden_part, hidden_other = collect_x(terms.astype(low))

    normed_terms, gain_terms = normed_grad(query_terms, grad_kv, weights, both)
    gain_rows = gain_terms.astype(low).reshape(-1, 2 * HEAD_DIM)
    depth = tok + gain_rows.shape[0]
    near = spread(jnp.concatenate([grad_kv, gain_rows], axis=0), "z")
    near = spread(near, "y").reshape(outer, depth, 2 * HEAD_DIM)
    rows = spread_x(rows)
    sums = kv_weight_grad(c.astype(jnp.int32)[None], rows, near, swap(near, "c"), tok)

    normed_part, normed_other = collect_x(normed_terms.reshape(NX, 2, rows_own, width))
    normed_other, hidden_other = hold(normed_other, hidden_other, sums)
    normed_other = swap(normed_other, "h")
    grad_normed = normed_part + normed_other.astype(wide)

    hidden_other = swap(hidden_other, "h")
    hidden_out = (stream_f + (hidden_part + hidden_other.astype(wide))).astype(low)

    sums = spread(sums, "x")
    grad_o, grad_q = weight_grads(rows, att_gq_all)
    sums = pairs(sums, grad_o)
    sums_other = swap(sums, "h")
    pair, other = sums[:, :block], sums_other[:, :block]
    gain_sum = sum_pair(sums[:, block:]) + sum_pair(sums_other[:, block:])
    grad_gain = gain_sum.reshape(width) / gain
    first, second = jnp.where(h == 0, pair, other), jnp.where(h == 0, other, pair)
    heads = [first[0], first[1], second[0], second[1]]
    grad_k, grad_v = (
        jnp.concatenate([a[:, i : i + HEAD_DIM] for a in heads], axis=1).astype(wide)
        for i in (0, HEAD_DIM)
    )

    scaled_grad = grad_normed * gain
    grad_stream = (
        inv_rms
        * (scaled_grad - unit_rows * jnp.mean(scaled_grad * unit_rows, axis=-1, keepdims=True))
        + grad_out.astype(wide)
    ).astype(low)
    return (hidden_out, grad_stream, grad_gain, grad_q, grad_k, grad_v, grad_o)


def solution(mesh):
    fine = Mesh(mesh.devices.reshape(tuple(SIZES.values())), tuple(SIZES))
    whole = P(DP + TENSOR, None)
    in_specs = (
        whole,
        P(TENSOR, DP, None),
        P(),
        P(DP, TENSOR),
        P(DP, None),
        P(DP, None),
        P(DP, TENSOR),
        whole,
        P(),
    )
    out_specs = (whole, whole, P(), P(DP, TENSOR), P(DP, None), P(DP, None), P(DP, TENSOR))
    return jax.shard_map(
        on_device, mesh=fine, in_specs=in_specs, out_specs=out_specs, check_vma=False
    )
```

```python
import jax
import jax.numpy as jnp
from jax import lax
from jax.experimental import pallas as pl
from jax.experimental.pallas import tpu as pltpu
from jax.sharding import Mesh
from jax.sharding import PartitionSpec as P

HEADS = 32
KV_HEADS = 4
HEAD_DIM = 128
HALF_DIM = HEAD_DIM // 2

eps = 1e-05
rope_base = 500000.0

SIZES = {"y": 4, "z": 4, "c": 2, "h": 2, "x": 4}
DP = ("y", "z", "c")
TENSOR = ("h", "x")
NX = SIZES["x"]
wide = jnp.float32
low = jnp.bfloat16


def dot(a, b, dims):
    return lax.dot_general(a, b, (dims, ((), ())), preferred_element_type=wide)


def swap(a, axis):
    return lax.ppermute(a, axis, [(0, 1), (1, 0)])


def shift(a, step):
    return lax.ppermute(a, "x", [((i + step) % NX, i) for i in range(NX)])


def spread(a, axis):
    size = SIZES[axis]
    return lax.all_to_all(
        jnp.broadcast_to(a[None], (size,) + a.shape), axis, 0, 0, tiled=True
    )


def collect(a, axis):
    return jnp.sum(lax.all_to_all(a, axis, 0, 0, tiled=True).astype(wide), axis=0)


def spread_h(a):
    return jnp.stack([a, swap(a, "h")])


def spread_x(a):
    return [a] + [shift(a, k) for k in range(1, NX)]


def sum_pair(a):
    return a[0].astype(wide) + a[1].astype(wide)


def collect_x(a):
    total = a[0].astype(wide)
    for k in range(1, NX):
        total = total + shift(a[k], NX - k).astype(wide)
    return total[0], total[1].astype(low)


def turn(field, cosine, sine):
    return field * cosine + pltpu.roll(field, HALF_DIM, 1) * sine


ANY = pl.BlockSpec(memory_space=pl.ANY)
PARAMS = pltpu.CompilerParams(vmem_limit_bytes=48 * 2**20)


def kv_project_kernel(normed, weights, cosine, sine, kv, total):
    step = pl.program_id(0)

    @pl.when(step == 0)
    def _():
        total[...] = jnp.zeros_like(total)

    total[...] += dot(normed[...], weights[...], ((1,), (0,)))

    @pl.when(step == pl.num_programs(0) - 1)
    def _():
        kv[:, :HEAD_DIM] = turn(total[:, :HEAD_DIM], cosine[...], sine[...]).astype(low)
        kv[:, HEAD_DIM:] = total[:, HEAD_DIM:].astype(low)


def kv_project(both, weights, cosine, sine, step=1024):
    tok = both.shape[0]
    width, cols = weights.shape
    kv_cols = 2 * HEAD_DIM
    fixed = pl.BlockSpec((tok, HEAD_DIM), lambda i: (0, 0))
    return pl.pallas_call(
        kv_project_kernel,
        grid=(width // step,),
        in_specs=[
            pl.BlockSpec((tok, step), lambda i: (0, i)),
            pl.BlockSpec((step, kv_cols), lambda i: (i, cols // kv_cols - 1)),
            fixed,
            fixed,
        ],
        out_specs=pl.BlockSpec((tok, kv_cols), lambda i: (0, 0)),
        out_shape=jax.ShapeDtypeStruct((tok, kv_cols), low),
        scratch_shapes=[pltpu.VMEM((tok, kv_cols), wide)],
        compiler_params=PARAMS,
    )(both, weights, cosine, sine)


def project_kernel(normed, grads, weights, cosine, sine, query, grad_heads, total):
    step = pl.program_id(0)
    tok, half = normed.shape[0], weights.shape[1] // 2

    @pl.when(step == 0)
    def _():
        total[...] = jnp.zeros_like(total)

    total[:, :half] += dot(normed[...], weights[:, :half], ((1,), (0,)))
    total[:, half:] += dot(grads[...], weights[:, half:], ((1,), (0,)))

    @pl.when(step == pl.num_programs(0) - 1)
    def _():
        for i in range(half // HEAD_DIM):
            at = pl.ds(i * tok, tok)
            query[at, :] = turn(
                total[:, i * HEAD_DIM : (i + 1) * HEAD_DIM], cosine[...], sine[...]
            ).astype(low)
            grad_heads[at, :] = total[
                :, half + i * HEAD_DIM : half + (i + 1) * HEAD_DIM
            ].astype(low)


def project(both, weights, cosine, sine, cols, step=1024):
    tok = both.shape[0]
    width = weights.shape[0]
    steps = width // step
    out = jax.ShapeDtypeStruct((cols // 2 // HEAD_DIM * tok, HEAD_DIM), low)
    fixed = pl.BlockSpec((tok, HEAD_DIM), lambda i: (0, 0))
    return pl.pallas_call(
        project_kernel,
        grid=(steps,),
        in_specs=[
            pl.BlockSpec((tok, step), lambda i: (0, i)),
            pl.BlockSpec((tok, step), lambda i: (0, i + steps)),
            pl.BlockSpec((step, cols), lambda i: (i, 0)),
            fixed,
            fixed,
        ],
        out_specs=[pl.BlockSpec(out.shape, lambda i: (0, 0))] * 2,
        out_shape=[out, out],
        scratch_shapes=[pltpu.VMEM((tok, cols), wide)],
        compiler_params=PARAMS,
    )(both, both, weights, cosine, sine)


def attend_kernel(
    at_chx,
    query,
    grad_heads,
    near,
    far,
    bounds,
    cosine,
    sine,
    att_gq,
    near_grad,
    far_grad,
    score,
):
    rows = query.shape[0]
    tok = cosine.shape[0]
    heads = rows // tok
    half = near.shape[0]
    step = 512
    scale = HEAD_DIM ** (-0.5)
    q, g = query[...], grad_heads[...]
    last, first = bounds[0:1, :], bounds[1:2, :]

    c, h, x = at_chx[0], at_chx[1], at_chx[2]
    key = lax.broadcasted_iota(jnp.int32, (step, tok), 0)
    key_x = (x + (key // 32) % NX) % NX
    key_h = (h + (key // 16) % 2) % 2
    local = (key // tok) * (2 * tok) + (key_h * NX + key_x) * 16 + key % 16

    peak = jnp.full((1, rows), -1e30, wide)
    for kv, base, core in ((near, 0, c), (far, half, 1 - c)):

        def mark(i, peak, kv=kv, base=base, core=core):
            at = pl.multiple_of(i * step, step)
            s = dot(kv[pl.ds(at, step), :HEAD_DIM], q, ((1,), (1,))) * scale
            place = local + (2 * at + core * tok)
            bias = jnp.where((place <= last) & (place >= first), 0.0, -1e30)
            s = s + jnp.concatenate([bias] * heads, axis=1)
            score[pl.ds(base + at, step), :] = s
            return jnp.maximum(peak, jnp.max(s, axis=0, keepdims=True))

        peak = lax.fori_loop(0, half // step, mark, peak)

    carry = (jnp.zeros((1, rows), wide), jnp.zeros((HEAD_DIM, rows), wide))
    for kv, base in ((near, 0), (far, half)):

        def weigh(i, carry, kv=kv, base=base):
            norm, out = carry
            at = pl.multiple_of(i * step, step)
            e = jnp.exp(score[pl.ds(base + at, step), :] - peak)
            score[pl.ds(base + at, step), :] = e
            out = out + dot(kv[pl.ds(at, step), HEAD_DIM:], e.astype(low), ((0,), (0,)))
            return norm + jnp.sum(e, axis=0, keepdims=True), out

        carry = lax.fori_loop(0, half // step, weigh, carry)
    norm, out = carry
    inverse = 1.0 / norm
    out = (out * inverse).astype(low).astype(wide)
    delta = jnp.sum(out * g.astype(wide).T, axis=0, keepdims=True)

    grad_query = jnp.zeros((HEAD_DIM, rows), wide)
    for kv, grad, base in ((near, near_grad, 0), (far, far_grad, half)):

        def back(i, grad_query, kv=kv, grad=grad, base=base):
            at = pl.multiple_of(i * step, step)
            p = score[pl.ds(base + at, step), :] * inverse
            gp = dot(kv[pl.ds(at, step), HEAD_DIM:], g, ((1,), (1,)))
            gs = (p * (gp - delta)).astype(low)
            grad[pl.ds(at, step), :HEAD_DIM] = (dot(gs, q, ((1,), (0,))) * scale).astype(low)
            grad[pl.ds(at, step), HEAD_DIM:] = dot(p.astype(low), g, ((1,), (0,))).astype(low)
            return grad_query + dot(kv[pl.ds(at, step), :HEAD_DIM], gs, ((0,), (0,)))

        grad_query = lax.fori_loop(0, half // step, back, grad_query)

    for i in range(heads):
        at, cols = slice(i * tok, (i + 1) * tok), slice(i * HEAD_DIM, (i + 1) * HEAD_DIM)
        att_gq[:, cols] = out[:, at].T.astype(low)
        back_cols = slice(heads * HEAD_DIM + cols.start, heads * HEAD_DIM + cols.stop)
        att_gq[:, back_cols] = turn(
            grad_query[:, at].T * scale, cosine[...], -sine[...]
        ).astype(low)


def attend(at_chx, query, grad_heads, near, far, bounds, cosine, sine):
    rows, tok = query.shape[0], cosine.shape[0]
    half = near.shape[0]
    vmem = pl.BlockSpec(memory_space=pltpu.VMEM)
    return pl.pallas_call(
        attend_kernel,
        in_specs=[pl.BlockSpec(memory_space=pltpu.SMEM)] + [vmem] * 7,
        out_shape=[
            jax.ShapeDtypeStruct((tok, 2 * rows // tok * HEAD_DIM), low),
            jax.ShapeDtypeStruct(near.shape, low),
            jax.ShapeDtypeStruct(far.shape, low),
        ],
        scratch_shapes=[pltpu.VMEM((2 * half, rows), wide)],
        compiler_params=PARAMS,
    )(at_chx, query, grad_heads, near, far, bounds, cosine, sine)


def back_project_kernel(att_gq, weights, waited, terms, grad):
    half = att_gq.shape[1] // 2
    terms[...] = dot(att_gq[:, :half], weights[:, half:], ((1,), (1,))).astype(low)
    grad[...] = dot(att_gq[:, half:], weights[:, :half], ((1,), (1,)))


def back_project(att_gq, weights, waited, step=1024):
    tok = att_gq.shape[0]
    width, cols = weights.shape[0], att_gq.shape[1]
    out = pl.BlockSpec((tok, step), lambda i: (0, i))
    return pl.pallas_call(
        back_project_kernel,
        grid=(width // step,),
        in_specs=[
            pl.BlockSpec(att_gq.shape, lambda i: (0, 0)),
            pl.BlockSpec((step, cols), lambda i: (i, 0)),
            ANY,
        ],
        out_specs=[out, out],
        out_shape=[
            jax.ShapeDtypeStruct((tok, width), low),
            jax.ShapeDtypeStruct((tok, width), wide),
        ],
        compiler_params=PARAMS,
    )(att_gq, weights, waited)


def normed_grad_kernel(query_terms, grad_kv, weights, normed, terms, gain):
    total = query_terms[...] + dot(grad_kv[...], weights[...], ((1,), (1,)))
    terms[...] = total.astype(low)
    gain[...] = jnp.sum(total * normed[...].astype(wide), axis=0, keepdims=True)


def normed_grad(query_terms, grad_kv, weights, both, step=1024):
    tok, width = query_terms.shape
    kv_cols = grad_kv.shape[1]
    at = weights.shape[1] // kv_cols - 1
    columns = pl.BlockSpec((tok, step), lambda i: (0, i))
    return pl.pallas_call(
        normed_grad_kernel,
        grid=(width // step,),
        in_specs=[
            columns,
            pl.BlockSpec((tok, kv_cols), lambda i: (0, 0)),
            pl.BlockSpec((step, kv_cols), lambda i: (i, at)),
            columns,
        ],
        out_specs=[columns, pl.BlockSpec((1, step), lambda i: (0, i))],
        out_shape=[
            jax.ShapeDtypeStruct((tok, width), low),
            jax.ShapeDtypeStruct((1, width), wide),
        ],
        compiler_params=PARAMS,
    )(query_terms, grad_kv, weights, both)


def positions(rows, at):
    return jnp.concatenate([part[j, at] for part in rows for j in range(2)], axis=0)


def weight_grad_kernel(*refs):
    rows, att_gq, grad_o, grad_q = refs[:NX], refs[NX], refs[-2], refs[-1]
    half, block = att_gq.shape[1] // 2, rows[0].shape[3] // 2

    @pl.when(pl.program_id(0) == 0)
    def _():
        grad_o[...] = jnp.zeros_like(grad_o)
        grad_q[...] = jnp.zeros_like(grad_q)

    own = jnp.concatenate([positions(rows, i) for i in range(rows[0].shape[1])], axis=0)
    grad_o[...] += dot(own[:, :block], att_gq[:, :half], ((0,), (0,)))
    grad_q[...] += dot(own[:, block:], att_gq[:, half:], ((0,), (0,)))


def weight_grads(rows, att_gq, step=8):
    two, n_dp, rows_own, both = rows[0].shape
    seq_len, cols = att_gq.shape
    out = jax.ShapeDtypeStruct((both // 2, cols // 2), wide)
    part = pl.BlockSpec((two, step, rows_own, both), lambda i: (0, i, 0, 0))
    return pl.pallas_call(
        weight_grad_kernel,
        grid=(n_dp // step,),
        in_specs=[part] * NX
        + [pl.BlockSpec((seq_len // n_dp * step, cols), lambda i: (i, 0))],
        out_specs=[pl.BlockSpec(out.shape, lambda i: (0, 0))] * 2,
        out_shape=[out, out],
        compiler_params=PARAMS,
    )(*rows, att_gq)


def kv_weight_grad_kernel(core, *refs):
    rows, (near, far, out, total, gains) = refs[:NX], refs[NX:]
    block = rows[0].shape[3] // 2
    tok = near.shape[1] - gains.shape[1]
    step = pl.program_id(0)

    @pl.when(step == 0)
    def _():
        total[...] = jnp.zeros_like(total)
        gains[...] = jnp.zeros_like(gains)

    c = core[0]
    for i in range(near.shape[0]):
        for at, (grad, of) in enumerate(((near, c), (far, 1 - c))):
            own = positions(rows, 2 * i + of)[:, block:]
            total[...] += dot(own, grad[i, :tok], ((0,), (0,)))
            gains[at] += grad[i, tok:].astype(wide)

    @pl.when(step == pl.num_programs(0) - 1)
    def _():
        out[: total.shape[0]] = total[...].astype(low)
        out[total.shape[0] :] = (gains[0] + gains[1]).astype(low)


def kv_weight_grad(core, rows, near, far, tok, step=4):
    two, n_dp, rows_own, both = rows[0].shape
    outer, depth, cols = near.shape
    kv = pl.BlockSpec((step, depth, cols), lambda i, c: (i, 0, 0))
    part = pl.BlockSpec((two, 2 * step, rows_own, both), lambda i, c: (0, i, 0, 0))
    out = jax.ShapeDtypeStruct((both // 2 + depth - tok, cols), low)
    return pl.pallas_call(
        kv_weight_grad_kernel,
        grid_spec=pltpu.PrefetchScalarGridSpec(
            num_scalar_prefetch=1,
            grid=(outer // step,),
            in_specs=[part] * NX + [kv, kv],
            out_specs=pl.BlockSpec(out.shape, lambda i, c: (0, 0)),
            scratch_shapes=[
                pltpu.VMEM((both // 2, cols), wide),
                pltpu.VMEM((2, depth - tok, cols), wide),
            ],
        ),
        out_shape=out,
        compiler_params=PARAMS,
    )(core, *rows, near, far)


def hold_kernel(first, second, waited, first_out, second_out):
    first_out[...] = first[...]
    second_out[...] = second[...]


def hold(first, second, waited):
    vmem = pl.BlockSpec(memory_space=pltpu.VMEM)
    return pl.pallas_call(
        hold_kernel,
        in_specs=[vmem, vmem, ANY],
        out_shape=[jax.ShapeDtypeStruct(a.shape, a.dtype) for a in (first, second)],
        compiler_params=PARAMS,
    )(first, second, waited)


def wait_kernel(value, waited, out):
    out[...] = value[...]


def wait(value, waited):
    return pl.pallas_call(
        wait_kernel,
        in_specs=[pl.BlockSpec(memory_space=pltpu.VMEM), ANY],
        out_shape=jax.ShapeDtypeStruct(value.shape, value.dtype),
        compiler_params=PARAMS,
    )(value, waited)


def pair_kernel(sums, waited, out):
    for i in range(2):
        out[i] = (sums[2 * i].astype(wide) + sums[2 * i + 1].astype(wide)).astype(low)


def pairs(sums, waited):
    return pl.pallas_call(
        pair_kernel,
        in_specs=[pl.BlockSpec(memory_space=pltpu.VMEM), ANY],
        out_shape=jax.ShapeDtypeStruct((NX // 2,) + sums.shape[1:], low),
        compiler_params=PARAMS,
    )(sums, waited)


def on_device(
    stream_in, pending, gain, q_weight, k_weight, v_weight, out_weight, grad_out, doc_ids
):
    y, z, c, h, x = (lax.axis_index(a) for a in ("y", "z", "c", "h", "x"))
    tens_index = h * NX + x
    rows_own, width = stream_in.shape
    tok = pending.shape[1]
    outer = SIZES["y"] * SIZES["z"]
    n_dp = outer * 2
    block = width // n_dp
    q_width = q_weight.shape[1]
    seq_len = doc_ids.shape[0]

    kv_first = tens_index * (q_width // HEAD_DIM) // (HEADS // KV_HEADS) * HEAD_DIM
    kv_weights = [
        lax.dynamic_slice_in_dim(w, kv_first, HEAD_DIM, 1) for w in (k_weight, v_weight)
    ]
    weights = lax.all_gather(
        jnp.concatenate([q_weight, out_weight], axis=1), DP, axis=0, tiled=True
    )
    near = spread(jnp.concatenate(kv_weights, axis=1), "z").reshape(-1, 2 * HEAD_DIM)
    near = spread(near, "y").reshape(outer, 1, block, 2 * HEAD_DIM)
    far = swap(near, "c")
    natural = [jnp.where(c == 0, near, far), jnp.where(c == 0, far, near)]
    wkv = jnp.concatenate(natural, axis=1).reshape(width, 2 * HEAD_DIM)

    stream_f = stream_in.astype(wide)
    inv_rms = lax.rsqrt(jnp.mean(stream_f * stream_f, axis=-1, keepdims=True) + eps)
    unit_rows = stream_f * inv_rms
    normed_own = (unit_rows * gain).astype(low)
    both = spread_h(jnp.concatenate([normed_own, grad_out], axis=1))
    both = jnp.stack(spread_x(both)).reshape(tok, 2 * width)

    split = [a.reshape(rows_own, n_dp, block) for a in (grad_out, normed_own)]
    rows = jnp.transpose(jnp.concatenate(split, axis=2), (1, 0, 2))

    def index(axis):
        return lax.broadcasted_iota(jnp.int32, (NX, 2, rows_own), axis)

    local = (((h ^ index(1)) * NX + (x + index(0)) % NX) * rows_own + index(2)).reshape(tok)
    block_first = ((y * SIZES["z"] + z) * 2 + c) * tok
    places = block_first + local
    def relative(a):
        a = a.reshape((2, NX, rows_own) + a.shape[1:])
        a = jnp.where(h == 0, a, a[::-1])
        a = lax.dynamic_slice_in_dim(jnp.concatenate([a, a], axis=1), x, NX, 1)
        return jnp.swapaxes(a, 0, 1)

    doc_query = relative(lax.dynamic_slice_in_dim(doc_ids, block_first, tok)).reshape(tok)
    first_place = jnp.sum((doc_ids[None, :] < doc_query[:, None]).astype(jnp.int32), axis=1)

    frequency = rope_base ** (-2.0 * jnp.arange(HALF_DIM).astype(wide) / HEAD_DIM)
    angles = places.astype(wide)[:, None] * frequency[None, :]
    cosine, sine = jnp.cos(angles), jnp.sin(angles)
    cosine = jnp.concatenate([cosine, cosine], axis=1)
    sine = jnp.concatenate([-sine, sine], axis=1)

    def rotate(field, sign):
        flipped = jnp.concatenate([field[:, HALF_DIM:], field[:, :HALF_DIM]], axis=1)
        return field * cosine + sign * flipped * sine

    pend = relative(pending[0])
    bounds = jnp.stack([places, first_place])
    both, pend, bounds, cosine, sine = lax.optimization_barrier(
        (both, pend, bounds, cosine, sine)
    )
    kv_own = kv_project(both, wkv, cosine, sine)
    kv_near = spread(kv_own, "z").reshape(-1, 2 * HEAD_DIM)
    query, grad_heads = project(both, weights, cosine, sine, 2 * q_width)
    kv_near = spread(kv_near, "y").reshape(-1, 2 * HEAD_DIM)
    kv_far = swap(kv_near, "c")
    rows = lax.all_to_all(wait(rows, kv_near), DP, 0, 0, tiled=True)
    at_chx = jnp.stack([c, h, x]).astype(jnp.int32)
    att_gq, near_piece, far_piece = attend(
        at_chx, query, grad_heads, kv_near, kv_far, bounds, cosine, sine
    )
    att_gq_all = lax.all_gather(wait(att_gq, rows), DP, axis=0, tiled=True)
    kv_sum = near_piece.astype(wide) + swap(far_piece, "c").astype(wide)
    kv_sum = kv_sum.astype(low).reshape(SIZES["y"], -1, 2 * HEAD_DIM)
    rows = wait(rows, kv_sum)
    rows = spread_h(rows)
    terms, query_terms = back_project(att_gq, weights, rows)
    kv_sum = collect(kv_sum, "y").astype(low)
    kv_grad = collect(kv_sum.reshape(SIZES["z"], tok, 2 * HEAD_DIM), "z")
    grad_key = rotate(kv_grad[:, :HEAD_DIM], -1.0)
    grad_kv = jnp.concatenate([grad_key, kv_grad[:, HEAD_DIM:]], axis=1).astype(low)

    terms = terms.reshape(NX, 2, rows_own, width).astype(wide) + pend.astype(wide)
    hidden_part, hidden_other = collect_x(terms.astype(low))

    normed_terms, gain_terms = normed_grad(query_terms, grad_kv, wkv, both)
    gain_rows = gain_terms.astype(low).reshape(-1, 2 * HEAD_DIM)
    depth = tok + gain_rows.shape[0]
    near = spread(jnp.concatenate([grad_kv, gain_rows], axis=0), "z")
    near = spread(near, "y").reshape(outer, depth, 2 * HEAD_DIM)
    rows = spread_x(rows)
    sums = kv_weight_grad(c.astype(jnp.int32)[None], rows, near, swap(near, "c"), tok)

    normed_part, normed_other = collect_x(normed_terms.reshape(NX, 2, rows_own, width))
    normed_other, hidden_other = hold(normed_other, hidden_other, sums)
    normed_other = swap(normed_other, "h")
    grad_normed = normed_part + normed_other.astype(wide)

    hidden_other = swap(hidden_other, "h")
    hidden_out = (stream_f + (hidden_part + hidden_other.astype(wide))).astype(low)

    sums = spread(sums, "x")
    grad_o, grad_q = weight_grads(rows, att_gq_all)
    sums = pairs(sums, grad_o)
    sums_other = swap(sums, "h")
    pair, other = sums[:, :block], sums_other[:, :block]
    gain_sum = sum_pair(sums[:, block:]) + sum_pair(sums_other[:, block:])
    grad_gain = gain_sum.reshape(width) / gain
    first, second = jnp.where(h == 0, pair, other), jnp.where(h == 0, other, pair)
    heads = [first[0], first[1], second[0], second[1]]
    grad_k, grad_v = (
        jnp.concatenate([a[:, i : i + HEAD_DIM] for a in heads], axis=1).astype(wide)
        for i in (0, HEAD_DIM)
    )

    scaled_grad = grad_normed * gain
    grad_stream = (
        inv_rms
        * (scaled_grad - unit_rows * jnp.mean(scaled_grad * unit_rows, axis=-1, keepdims=True))
        + grad_out.astype(wide)
    ).astype(low)
    return (hidden_out, grad_stream, grad_gain, grad_q, grad_k, grad_v, grad_o)


def solution(mesh):
    fine = Mesh(mesh.devices.reshape(tuple(SIZES.values())), tuple(SIZES))
    whole = P(DP + TENSOR, None)
    in_specs = (
        whole,
        P(TENSOR, DP, None),
        P(),
        P(DP, TENSOR),
        P(DP, None),
        P(DP, None),
        P(DP, TENSOR),
        whole,
        P(),
    )
    out_specs = (whole, whole, P(), P(DP, TENSOR), P(DP, None), P(DP, None), P(DP, TENSOR))
    return jax.shard_map(
        on_device, mesh=fine, in_specs=in_specs, out_specs=out_specs, check_vma=False
    )
```

```python
import jax
import jax.numpy as jnp
from jax import lax
from jax.experimental import pallas as pl
from jax.experimental.pallas import tpu as pltpu
from jax.sharding import Mesh
from jax.sharding import PartitionSpec as P

HEADS = 32
KV_HEADS = 4
HEAD_DIM = 128
HALF_DIM = HEAD_DIM // 2

eps = 1e-05
rope_base = 500000.0

SIZES = {"y": 4, "z": 4, "c": 2, "h": 2, "x": 4}
DP = ("y", "z", "c")
TENSOR = ("h", "x")
NX = SIZES["x"]
wide = jnp.float32
low = jnp.bfloat16


def dot(a, b, dims):
    return lax.dot_general(a, b, (dims, ((), ())), preferred_element_type=wide)


def swap(a, axis):
    return lax.ppermute(a, axis, [(0, 1), (1, 0)])


def shift(a, step):
    return lax.ppermute(a, "x", [((i + step) % NX, i) for i in range(NX)])


def spread(a, axis):
    size = SIZES[axis]
    return lax.all_to_all(
        jnp.broadcast_to(a[None], (size,) + a.shape), axis, 0, 0, tiled=True
    )


def collect(a, axis):
    return jnp.sum(lax.all_to_all(a, axis, 0, 0, tiled=True).astype(wide), axis=0)


def spread_h(a):
    return jnp.stack([a, swap(a, "h")])


def spread_x(a):
    return [a] + [shift(a, k) for k in range(1, NX)]


def sum_pair(a):
    return a[0].astype(wide) + a[1].astype(wide)


def collect_x(a):
    total = a[0].astype(wide)
    for k in range(1, NX):
        total = total + shift(a[k], NX - k).astype(wide)
    return total[0], total[1].astype(low)


def turn(field, cosine, sine):
    return field * cosine + pltpu.roll(field, HALF_DIM, 1) * sine


ANY = pl.BlockSpec(memory_space=pl.ANY)
PARAMS = pltpu.CompilerParams(vmem_limit_bytes=48 * 2**20)


def kv_project_kernel(normed, weights, cosine, sine, kv, total):
    step = pl.program_id(0)

    @pl.when(step == 0)
    def _():
        total[...] = jnp.zeros_like(total)

    total[...] += dot(normed[...], weights[...], ((1,), (0,)))

    @pl.when(step == pl.num_programs(0) - 1)
    def _():
        kv[:, :HEAD_DIM] = turn(total[:, :HEAD_DIM], cosine[...], sine[...]).astype(low)
        kv[:, HEAD_DIM:] = total[:, HEAD_DIM:].astype(low)


def kv_project(both, weights, cosine, sine, step=1024):
    tok = both.shape[0]
    width, cols = weights.shape
    kv_cols = 2 * HEAD_DIM
    fixed = pl.BlockSpec((tok, HEAD_DIM), lambda i: (0, 0))
    return pl.pallas_call(
        kv_project_kernel,
        grid=(width // step,),
        in_specs=[
            pl.BlockSpec((tok, step), lambda i: (0, i)),
            pl.BlockSpec((step, kv_cols), lambda i: (i, cols // kv_cols - 1)),
            fixed,
            fixed,
        ],
        out_specs=pl.BlockSpec((tok, kv_cols), lambda i: (0, 0)),
        out_shape=jax.ShapeDtypeStruct((tok, kv_cols), low),
        scratch_shapes=[pltpu.VMEM((tok, kv_cols), wide)],
        compiler_params=PARAMS,
    )(both, weights, cosine, sine)


def project_kernel(normed, grads, weights, cosine, sine, query, grad_heads, total):
    step = pl.program_id(0)
    tok, half = normed.shape[0], weights.shape[1] // 2

    @pl.when(step == 0)
    def _():
        total[...] = jnp.zeros_like(total)

    total[:, :half] += dot(normed[...], weights[:, :half], ((1,), (0,)))
    total[:, half:] += dot(grads[...], weights[:, half:], ((1,), (0,)))

    @pl.when(step == pl.num_programs(0) - 1)
    def _():
        for i in range(half // HEAD_DIM):
            at = pl.ds(i * tok, tok)
            query[at, :] = turn(
                total[:, i * HEAD_DIM : (i + 1) * HEAD_DIM], cosine[...], sine[...]
            ).astype(low)
            grad_heads[at, :] = total[
                :, half + i * HEAD_DIM : half + (i + 1) * HEAD_DIM
            ].astype(low)


def project(both, weights, cosine, sine, cols, step=1024):
    tok = both.shape[0]
    width = weights.shape[0]
    steps = width // step
    out = jax.ShapeDtypeStruct((cols // 2 // HEAD_DIM * tok, HEAD_DIM), low)
    fixed = pl.BlockSpec((tok, HEAD_DIM), lambda i: (0, 0))
    return pl.pallas_call(
        project_kernel,
        grid=(steps,),
        in_specs=[
            pl.BlockSpec((tok, step), lambda i: (0, i)),
            pl.BlockSpec((tok, step), lambda i: (0, i + steps)),
            pl.BlockSpec((step, cols), lambda i: (i, 0)),
            fixed,
            fixed,
        ],
        out_specs=[pl.BlockSpec(out.shape, lambda i: (0, 0))] * 2,
        out_shape=[out, out],
        scratch_shapes=[pltpu.VMEM((tok, cols), wide)],
        compiler_params=PARAMS,
    )(both, both, weights, cosine, sine)


def attend_kernel(
    at_chx,
    query,
    grad_heads,
    near,
    far,
    bounds,
    cosine,
    sine,
    att_gq,
    near_grad,
    far_grad,
    score,
):
    rows = query.shape[0]
    tok = cosine.shape[0]
    heads = rows // tok
    half = near.shape[0]
    step = 512
    scale = HEAD_DIM ** (-0.5)
    q, g = query[...], grad_heads[...]
    last, first = bounds[0:1, :], bounds[1:2, :]

    c, h, x = at_chx[0], at_chx[1], at_chx[2]
    key = lax.broadcasted_iota(jnp.int32, (step, tok), 0)
    key_x = (x + (key // 32) % NX) % NX
    key_h = (h + (key // 16) % 2) % 2
    local = (key // tok) * (2 * tok) + (key_h * NX + key_x) * 16 + key % 16

    peak = jnp.full((1, rows), -1e30, wide)
    for kv, base, core in ((near, 0, c), (far, half, 1 - c)):

        def mark(i, peak, kv=kv, base=base, core=core):
            at = pl.multiple_of(i * step, step)
            s = dot(kv[pl.ds(at, step), :HEAD_DIM], q, ((1,), (1,))) * scale
            place = local + (2 * at + core * tok)
            bias = jnp.where((place <= last) & (place >= first), 0.0, -1e30)
            s = s + jnp.concatenate([bias] * heads, axis=1)
            score[pl.ds(base + at, step), :] = s
            return jnp.maximum(peak, jnp.max(s, axis=0, keepdims=True))

        peak = lax.fori_loop(0, half // step, mark, peak)

    carry = (jnp.zeros((1, rows), wide), jnp.zeros((HEAD_DIM, rows), wide))
    for kv, base in ((near, 0), (far, half)):

        def weigh(i, carry, kv=kv, base=base):
            norm, out = carry
            at = pl.multiple_of(i * step, step)
            e = jnp.exp(score[pl.ds(base + at, step), :] - peak)
            score[pl.ds(base + at, step), :] = e
            out = out + dot(kv[pl.ds(at, step), HEAD_DIM:], e.astype(low), ((0,), (0,)))
            return norm + jnp.sum(e, axis=0, keepdims=True), out

        carry = lax.fori_loop(0, half // step, weigh, carry)
    norm, out = carry
    inverse = 1.0 / norm
    out = (out * inverse).astype(low).astype(wide)
    delta = jnp.sum(out * g.astype(wide).T, axis=0, keepdims=True)

    grad_query = jnp.zeros((HEAD_DIM, rows), wide)
    for kv, grad, base in ((near, near_grad, 0), (far, far_grad, half)):

        def back(i, grad_query, kv=kv, grad=grad, base=base):
            at = pl.multiple_of(i * step, step)
            p = score[pl.ds(base + at, step), :] * inverse
            gp = dot(kv[pl.ds(at, step), HEAD_DIM:], g, ((1,), (1,)))
            gs = (p * (gp - delta)).astype(low)
            grad[pl.ds(at, step), :HEAD_DIM] = (dot(gs, q, ((1,), (0,))) * scale).astype(low)
            grad[pl.ds(at, step), HEAD_DIM:] = dot(p.astype(low), g, ((1,), (0,))).astype(low)
            return grad_query + dot(kv[pl.ds(at, step), :HEAD_DIM], gs, ((0,), (0,)))

        grad_query = lax.fori_loop(0, half // step, back, grad_query)

    for i in range(heads):
        at, cols = slice(i * tok, (i + 1) * tok), slice(i * HEAD_DIM, (i + 1) * HEAD_DIM)
        att_gq[:, cols] = out[:, at].T.astype(low)
        back_cols = slice(heads * HEAD_DIM + cols.start, heads * HEAD_DIM + cols.stop)
        att_gq[:, back_cols] = turn(
            grad_query[:, at].T * scale, cosine[...], -sine[...]
        ).astype(low)


def attend(at_chx, query, grad_heads, near, far, bounds, cosine, sine):
    rows, tok = query.shape[0], cosine.shape[0]
    half = near.shape[0]
    vmem = pl.BlockSpec(memory_space=pltpu.VMEM)
    return pl.pallas_call(
        attend_kernel,
        in_specs=[pl.BlockSpec(memory_space=pltpu.SMEM)] + [vmem] * 7,
        out_shape=[
            jax.ShapeDtypeStruct((tok, 2 * rows // tok * HEAD_DIM), low),
            jax.ShapeDtypeStruct(near.shape, low),
            jax.ShapeDtypeStruct(far.shape, low),
        ],
        scratch_shapes=[pltpu.VMEM((2 * half, rows), wide)],
        compiler_params=PARAMS,
    )(at_chx, query, grad_heads, near, far, bounds, cosine, sine)


def back_project_kernel(att_gq, weights, waited, terms, grad):
    half = att_gq.shape[1] // 2
    terms[...] = dot(att_gq[:, :half], weights[:, half:], ((1,), (1,))).astype(low)
    grad[...] = dot(att_gq[:, half:], weights[:, :half], ((1,), (1,))).astype(low)


def back_project(att_gq, weights, waited, step=1024):
    tok = att_gq.shape[0]
    width, cols = weights.shape[0], att_gq.shape[1]
    out = pl.BlockSpec((tok, step), lambda i: (0, i))
    return pl.pallas_call(
        back_project_kernel,
        grid=(width // step,),
        in_specs=[
            pl.BlockSpec(att_gq.shape, lambda i: (0, 0)),
            pl.BlockSpec((step, cols), lambda i: (i, 0)),
            ANY,
        ],
        out_specs=[out, out],
        out_shape=[
            jax.ShapeDtypeStruct((tok, width), low),
            jax.ShapeDtypeStruct((tok, width), low),
        ],
        compiler_params=PARAMS,
    )(att_gq, weights, waited)


def normed_grad_kernel(query_terms, grad_kv, weights, normed, terms, gain):
    total = query_terms[...].astype(wide) + dot(grad_kv[...], weights[...], ((1,), (1,)))
    terms[...] = total.astype(low)
    gain[...] = jnp.sum(total * normed[...].astype(wide), axis=0, keepdims=True)


def normed_grad(query_terms, grad_kv, weights, both, step=1024):
    tok, width = query_terms.shape
    kv_cols = grad_kv.shape[1]
    at = weights.shape[1] // kv_cols - 1
    columns = pl.BlockSpec((tok, step), lambda i: (0, i))
    return pl.pallas_call(
        normed_grad_kernel,
        grid=(width // step,),
        in_specs=[
            columns,
            pl.BlockSpec((tok, kv_cols), lambda i: (0, 0)),
            pl.BlockSpec((step, kv_cols), lambda i: (i, at)),
            columns,
        ],
        out_specs=[columns, pl.BlockSpec((1, step), lambda i: (0, i))],
        out_shape=[
            jax.ShapeDtypeStruct((tok, width), low),
            jax.ShapeDtypeStruct((1, width), wide),
        ],
        compiler_params=PARAMS,
    )(query_terms, grad_kv, weights, both)


def positions(rows, at):
    return jnp.concatenate([part[j, at] for part in rows for j in range(2)], axis=0)


def weight_grad_kernel(*refs):
    rows, att_gq, grad_o, grad_q = refs[:NX], refs[NX], refs[-2], refs[-1]
    half, block = att_gq.shape[1] // 2, rows[0].shape[3] // 2

    @pl.when(pl.program_id(0) == 0)
    def _():
        grad_o[...] = jnp.zeros_like(grad_o)
        grad_q[...] = jnp.zeros_like(grad_q)

    own = jnp.concatenate([positions(rows, i) for i in range(rows[0].shape[1])], axis=0)
    grad_o[...] += dot(own[:, :block], att_gq[:, :half], ((0,), (0,)))
    grad_q[...] += dot(own[:, block:], att_gq[:, half:], ((0,), (0,)))


def weight_grads(rows, att_gq, step=8):
    two, n_dp, rows_own, both = rows[0].shape
    seq_len, cols = att_gq.shape
    out = jax.ShapeDtypeStruct((both // 2, cols // 2), wide)
    part = pl.BlockSpec((two, step, rows_own, both), lambda i: (0, i, 0, 0))
    return pl.pallas_call(
        weight_grad_kernel,
        grid=(n_dp // step,),
        in_specs=[part] * NX
        + [pl.BlockSpec((seq_len // n_dp * step, cols), lambda i: (i, 0))],
        out_specs=[pl.BlockSpec(out.shape, lambda i: (0, 0))] * 2,
        out_shape=[out, out],
        compiler_params=PARAMS,
    )(*rows, att_gq)


def kv_weight_grad_kernel(core, *refs):
    rows, (near, far, _, out, total, gains) = refs[:NX], refs[NX:]
    block = rows[0].shape[3] // 2
    tok = near.shape[1] - gains.shape[1]
    step = pl.program_id(0)

    @pl.when(step == 0)
    def _():
        total[...] = jnp.zeros_like(total)
        gains[...] = jnp.zeros_like(gains)

    c = core[0]
    for i in range(near.shape[0]):
        for at, (grad, of) in enumerate(((near, c), (far, 1 - c))):
            own = positions(rows, 2 * i + of)[:, block:]
            total[...] += dot(own, grad[i, :tok], ((0,), (0,)))
            gains[at] += grad[i, tok:].astype(wide)

    @pl.when(step == pl.num_programs(0) - 1)
    def _():
        out[: total.shape[0]] = total[...].astype(low)
        out[total.shape[0] :] = (gains[0] + gains[1]).astype(low)


def kv_weight_grad(core, rows, near, far, waited, tok, step=4):
    two, n_dp, rows_own, both = rows[0].shape
    outer, depth, cols = near.shape
    kv = pl.BlockSpec((step, depth, cols), lambda i, c: (i, 0, 0))
    part = pl.BlockSpec((two, 2 * step, rows_own, both), lambda i, c: (0, i, 0, 0))
    out = jax.ShapeDtypeStruct((both // 2 + depth - tok, cols), low)
    return pl.pallas_call(
        kv_weight_grad_kernel,
        grid_spec=pltpu.PrefetchScalarGridSpec(
            num_scalar_prefetch=1,
            grid=(outer // step,),
            in_specs=[part] * NX + [kv, kv, ANY],
            out_specs=pl.BlockSpec(out.shape, lambda i, c: (0, 0)),
            scratch_shapes=[
                pltpu.VMEM((both // 2, cols), wide),
                pltpu.VMEM((2, depth - tok, cols), wide),
            ],
        ),
        out_shape=out,
        compiler_params=PARAMS,
    )(core, *rows, near, far, waited)


def wait_kernel(value, waited, out):
    out[...] = value[...]


def wait(value, waited):
    return pl.pallas_call(
        wait_kernel,
        in_specs=[pl.BlockSpec(memory_space=pltpu.VMEM), ANY],
        out_shape=jax.ShapeDtypeStruct(value.shape, value.dtype),
        compiler_params=PARAMS,
    )(value, waited)


def pair_kernel(sums, waited, out):
    for i in range(2):
        out[i] = (sums[2 * i].astype(wide) + sums[2 * i + 1].astype(wide)).astype(low)


def pairs(sums, waited):
    return pl.pallas_call(
        pair_kernel,
        in_specs=[pl.BlockSpec(memory_space=pltpu.VMEM), ANY],
        out_shape=jax.ShapeDtypeStruct((NX // 2,) + sums.shape[1:], low),
        compiler_params=PARAMS,
    )(sums, waited)


def on_device(
    stream_in, pending, gain, q_weight, k_weight, v_weight, out_weight, grad_out, doc_ids
):
    y, z, c, h, x = (lax.axis_index(a) for a in ("y", "z", "c", "h", "x"))
    tens_index = h * NX + x
    rows_own, width = stream_in.shape
    tok = pending.shape[1]
    outer = SIZES["y"] * SIZES["z"]
    n_dp = outer * 2
    block = width // n_dp
    q_width = q_weight.shape[1]
    seq_len = doc_ids.shape[0]

    kv_first = tens_index * (q_width // HEAD_DIM) // (HEADS // KV_HEADS) * HEAD_DIM
    kv_weights = [
        lax.dynamic_slice_in_dim(w, kv_first, HEAD_DIM, 1) for w in (k_weight, v_weight)
    ]
    weights = lax.all_gather(
        jnp.concatenate([q_weight, out_weight], axis=1), DP, axis=0, tiled=True
    )
    near = spread(jnp.concatenate(kv_weights, axis=1), "z").reshape(-1, 2 * HEAD_DIM)
    near = spread(near, "y").reshape(outer, 1, block, 2 * HEAD_DIM)
    far = swap(near, "c")
    natural = [jnp.where(c == 0, near, far), jnp.where(c == 0, far, near)]
    wkv = jnp.concatenate(natural, axis=1).reshape(width, 2 * HEAD_DIM)

    stream_f = stream_in.astype(wide)
    inv_rms = lax.rsqrt(jnp.mean(stream_f * stream_f, axis=-1, keepdims=True) + eps)
    unit_rows = stream_f * inv_rms
    normed_own = (unit_rows * gain).astype(low)
    both = spread_h(jnp.concatenate([normed_own, grad_out], axis=1))
    both = jnp.stack(spread_x(both)).reshape(tok, 2 * width)

    split = [a.reshape(rows_own, n_dp, block) for a in (grad_out, normed_own)]
    rows = jnp.transpose(jnp.concatenate(split, axis=2), (1, 0, 2))

    def index(axis):
        return lax.broadcasted_iota(jnp.int32, (NX, 2, rows_own), axis)

    local = (((h ^ index(1)) * NX + (x + index(0)) % NX) * rows_own + index(2)).reshape(tok)
    block_first = ((y * SIZES["z"] + z) * 2 + c) * tok
    places = block_first + local
    def relative(a):
        a = a.reshape((2, NX, rows_own) + a.shape[1:])
        a = jnp.where(h == 0, a, a[::-1])
        a = lax.dynamic_slice_in_dim(jnp.concatenate([a, a], axis=1), x, NX, 1)
        return jnp.swapaxes(a, 0, 1)

    doc_query = relative(lax.dynamic_slice_in_dim(doc_ids, block_first, tok)).reshape(tok)
    first_place = jnp.sum((doc_ids[None, :] < doc_query[:, None]).astype(jnp.int32), axis=1)

    frequency = rope_base ** (-2.0 * jnp.arange(HALF_DIM).astype(wide) / HEAD_DIM)
    angles = places.astype(wide)[:, None] * frequency[None, :]
    cosine, sine = jnp.cos(angles), jnp.sin(angles)
    cosine = jnp.concatenate([cosine, cosine], axis=1)
    sine = jnp.concatenate([-sine, sine], axis=1)

    def rotate(field, sign):
        flipped = jnp.concatenate([field[:, HALF_DIM:], field[:, :HALF_DIM]], axis=1)
        return field * cosine + sign * flipped * sine

    pend = relative(pending[0])
    bounds = jnp.stack([places, first_place])
    both, pend, bounds, cosine, sine = lax.optimization_barrier(
        (both, pend, bounds, cosine, sine)
    )
    kv_own = kv_project(both, wkv, cosine, sine)
    kv_near = spread(kv_own, "z").reshape(-1, 2 * HEAD_DIM)
    query, grad_heads = project(both, weights, cosine, sine, 2 * q_width)
    kv_near = spread(kv_near, "y").reshape(-1, 2 * HEAD_DIM)
    kv_far = swap(kv_near, "c")
    rows = lax.all_to_all(wait(rows, kv_near), DP, 0, 0, tiled=True)
    at_chx = jnp.stack([c, h, x]).astype(jnp.int32)
    att_gq, near_piece, far_piece = attend(
        at_chx, query, grad_heads, kv_near, kv_far, bounds, cosine, sine
    )
    att_gq_all = lax.all_gather(wait(att_gq, rows), DP, axis=0, tiled=True)
    kv_sum = near_piece.astype(wide) + swap(far_piece, "c").astype(wide)
    kv_sum = kv_sum.astype(low).reshape(SIZES["y"], -1, 2 * HEAD_DIM)
    rows = wait(rows, kv_sum)
    rows = spread_h(rows)
    terms, query_terms = back_project(att_gq, weights, rows)
    kv_sum = collect(kv_sum, "y").astype(low)
    kv_grad = collect(kv_sum.reshape(SIZES["z"], tok, 2 * HEAD_DIM), "z")
    grad_key = rotate(kv_grad[:, :HEAD_DIM], -1.0)
    grad_kv = jnp.concatenate([grad_key, kv_grad[:, HEAD_DIM:]], axis=1).astype(low)

    terms = terms.reshape(NX, 2, rows_own, width).astype(wide) + pend.astype(wide)
    hidden_part, hidden_other = collect_x(terms.astype(low))

    normed_terms, gain_terms = normed_grad(query_terms, grad_kv, wkv, both)
    gain_rows = gain_terms.astype(low).reshape(-1, 2 * HEAD_DIM)
    depth = tok + gain_rows.shape[0]
    near = spread(jnp.concatenate([grad_kv, gain_rows], axis=0), "z")
    near = spread(near, "y").reshape(outer, depth, 2 * HEAD_DIM)
    rows = spread_x(rows)
    hidden_other = swap(hidden_other, "h")
    sums = kv_weight_grad(
        c.astype(jnp.int32)[None], rows, near, swap(near, "c"), hidden_other, tok
    )

    normed_part, normed_other = collect_x(normed_terms.reshape(NX, 2, rows_own, width))
    normed_other = swap(wait(normed_other, sums), "h")
    grad_normed = normed_part + normed_other.astype(wide)
    hidden_out = (stream_f + (hidden_part + hidden_other.astype(wide))).astype(low)

    sums = spread(sums, "x")
    grad_o, grad_q = weight_grads(rows, att_gq_all)
    sums = pairs(sums, grad_o)
    sums_other = swap(sums, "h")
    pair, other = sums[:, :block], sums_other[:, :block]
    gain_sum = sum_pair(sums[:, block:]) + sum_pair(sums_other[:, block:])
    grad_gain = gain_sum.reshape(width) / gain
    first, second = jnp.where(h == 0, pair, other), jnp.where(h == 0, other, pair)
    heads = [first[0], first[1], second[0], second[1]]
    grad_k, grad_v = (
        jnp.concatenate([a[:, i : i + HEAD_DIM] for a in heads], axis=1).astype(wide)
        for i in (0, HEAD_DIM)
    )

    scaled_grad = grad_normed * gain
    grad_stream = (
        inv_rms
        * (scaled_grad - unit_rows * jnp.mean(scaled_grad * unit_rows, axis=-1, keepdims=True))
        + grad_out.astype(wide)
    ).astype(low)
    return (hidden_out, grad_stream, grad_gain, grad_q, grad_k, grad_v, grad_o)


def solution(mesh):
    fine = Mesh(mesh.devices.reshape(tuple(SIZES.values())), tuple(SIZES))
    whole = P(DP + TENSOR, None)
    in_specs = (
        whole,
        P(TENSOR, DP, None),
        P(),
        P(DP, TENSOR),
        P(DP, None),
        P(DP, None),
        P(DP, TENSOR),
        whole,
        P(),
    )
    out_specs = (whole, whole, P(), P(DP, TENSOR), P(DP, None), P(DP, None), P(DP, TENSOR))
    return jax.shard_map(
        on_device, mesh=fine, in_specs=in_specs, out_specs=out_specs, check_vma=False
    )
```

```python
import jax
import jax.numpy as jnp
from jax import lax
from jax.experimental import pallas as pl
from jax.experimental.pallas import tpu as pltpu
from jax.sharding import Mesh
from jax.sharding import PartitionSpec as P

HEADS = 32
KV_HEADS = 4
HEAD_DIM = 128
HALF_DIM = HEAD_DIM // 2

eps = 1e-05
rope_base = 500000.0

SIZES = {"y": 4, "z": 4, "c": 2, "h": 2, "x": 4}
DP = ("y", "z", "c")
TENSOR = ("h", "x")
NX = SIZES["x"]
wide = jnp.float32
low = jnp.bfloat16


def dot(a, b, dims):
    return lax.dot_general(a, b, (dims, ((), ())), preferred_element_type=wide)


def swap(a, axis):
    return lax.ppermute(a, axis, [(0, 1), (1, 0)])


def shift(a, step):
    return lax.ppermute(a, "x", [((i + step) % NX, i) for i in range(NX)])


def spread(a, axis):
    size = SIZES[axis]
    return lax.all_to_all(
        jnp.broadcast_to(a[None], (size,) + a.shape), axis, 0, 0, tiled=True
    )


def collect(a, axis):
    return jnp.sum(lax.all_to_all(a, axis, 0, 0, tiled=True).astype(wide), axis=0)


def spread_h(a):
    return jnp.stack([a, swap(a, "h")])


def spread_x(a):
    return [a] + [shift(a, k) for k in range(1, NX)]


def sum_pair(a):
    return a[0].astype(wide) + a[1].astype(wide)


def collect_x(a):
    total = a[0].astype(wide)
    for k in range(1, NX):
        total = total + shift(a[k], NX - k).astype(wide)
    return total[0], total[1].astype(low)


def turn(field, cosine, sine):
    return field * cosine + pltpu.roll(field, HALF_DIM, 1) * sine


ANY = pl.BlockSpec(memory_space=pl.ANY)
PARAMS = pltpu.CompilerParams(vmem_limit_bytes=48 * 2**20)


def kv_project_kernel(normed, weights, cosine, sine, kv, total):
    step = pl.program_id(0)

    @pl.when(step == 0)
    def _():
        total[...] = jnp.zeros_like(total)

    total[...] += dot(normed[...], weights[...], ((1,), (0,)))

    @pl.when(step == pl.num_programs(0) - 1)
    def _():
        kv[:, :HEAD_DIM] = turn(total[:, :HEAD_DIM], cosine[...], sine[...]).astype(low)
        kv[:, HEAD_DIM:] = total[:, HEAD_DIM:].astype(low)


def kv_project(both, weights, cosine, sine, step=1024):
    tok = both.shape[0]
    width, cols = weights.shape
    kv_cols = 2 * HEAD_DIM
    fixed = pl.BlockSpec((tok, HEAD_DIM), lambda i: (0, 0))
    return pl.pallas_call(
        kv_project_kernel,
        grid=(width // step,),
        in_specs=[
            pl.BlockSpec((tok, step), lambda i: (0, i)),
            pl.BlockSpec((step, kv_cols), lambda i: (i, cols // kv_cols - 1)),
            fixed,
            fixed,
        ],
        out_specs=pl.BlockSpec((tok, kv_cols), lambda i: (0, 0)),
        out_shape=jax.ShapeDtypeStruct((tok, kv_cols), low),
        scratch_shapes=[pltpu.VMEM((tok, kv_cols), wide)],
        compiler_params=PARAMS,
    )(both, weights, cosine, sine)


def project_kernel(normed, grads, weights, cosine, sine, query, grad_heads, total):
    step = pl.program_id(0)
    tok, half = normed.shape[0], weights.shape[1] // 2

    @pl.when(step == 0)
    def _():
        total[...] = jnp.zeros_like(total)

    total[:, :half] += dot(normed[...], weights[:, :half], ((1,), (0,)))
    total[:, half:] += dot(grads[...], weights[:, half:], ((1,), (0,)))

    @pl.when(step == pl.num_programs(0) - 1)
    def _():
        for i in range(half // HEAD_DIM):
            at = pl.ds(i * tok, tok)
            query[at, :] = turn(
                total[:, i * HEAD_DIM : (i + 1) * HEAD_DIM], cosine[...], sine[...]
            ).astype(low)
            grad_heads[at, :] = total[
                :, half + i * HEAD_DIM : half + (i + 1) * HEAD_DIM
            ].astype(low)


def project(both, weights, cosine, sine, cols, step=1024):
    tok = both.shape[0]
    width = weights.shape[0]
    steps = width // step
    out = jax.ShapeDtypeStruct((cols // 2 // HEAD_DIM * tok, HEAD_DIM), low)
    fixed = pl.BlockSpec((tok, HEAD_DIM), lambda i: (0, 0))
    return pl.pallas_call(
        project_kernel,
        grid=(steps,),
        in_specs=[
            pl.BlockSpec((tok, step), lambda i: (0, i)),
            pl.BlockSpec((tok, step), lambda i: (0, i + steps)),
            pl.BlockSpec((step, cols), lambda i: (i, 0)),
            fixed,
            fixed,
        ],
        out_specs=[pl.BlockSpec(out.shape, lambda i: (0, 0))] * 2,
        out_shape=[out, out],
        scratch_shapes=[pltpu.VMEM((tok, cols), wide)],
        compiler_params=PARAMS,
    )(both, both, weights, cosine, sine)


def attend_kernel(
    at_chx,
    query,
    grad_heads,
    near,
    far,
    bounds,
    cosine,
    sine,
    att_gq,
    near_grad,
    far_grad,
    score,
):
    rows = query.shape[0]
    tok = cosine.shape[0]
    heads = rows // tok
    half = near.shape[0]
    step = 512
    scale = HEAD_DIM ** (-0.5)
    q, g = query[...], grad_heads[...]
    last, first = bounds[0:1, :], bounds[1:2, :]

    c, h, x = at_chx[0], at_chx[1], at_chx[2]
    key = lax.broadcasted_iota(jnp.int32, (step, tok), 0)
    key_x = (x + (key // 32) % NX) % NX
    key_h = (h + (key // 16) % 2) % 2
    local = (key // tok) * (2 * tok) + (key_h * NX + key_x) * 16 + key % 16

    peak = jnp.full((1, rows), -1e30, wide)
    for kv, base, core in ((near, 0, c), (far, half, 1 - c)):

        def mark(i, peak, kv=kv, base=base, core=core):
            at = pl.multiple_of(i * step, step)
            s = dot(kv[pl.ds(at, step), :HEAD_DIM], q, ((1,), (1,))) * scale
            place = local + (2 * at + core * tok)
            bias = jnp.where((place <= last) & (place >= first), 0.0, -1e30)
            s = s + jnp.concatenate([bias] * heads, axis=1)
            score[pl.ds(base + at, step), :] = s
            return jnp.maximum(peak, jnp.max(s, axis=0, keepdims=True))

        peak = lax.fori_loop(0, half // step, mark, peak, unroll=True)

    carry = (jnp.zeros((1, rows), wide), jnp.zeros((HEAD_DIM, rows), wide))
    for kv, base in ((near, 0), (far, half)):

        def weigh(i, carry, kv=kv, base=base):
            norm, out = carry
            at = pl.multiple_of(i * step, step)
            e = jnp.exp(score[pl.ds(base + at, step), :] - peak)
            score[pl.ds(base + at, step), :] = e
            out = out + dot(kv[pl.ds(at, step), HEAD_DIM:], e.astype(low), ((0,), (0,)))
            return norm + jnp.sum(e, axis=0, keepdims=True), out

        carry = lax.fori_loop(0, half // step, weigh, carry, unroll=True)
    norm, out = carry
    inverse = 1.0 / norm
    out = (out * inverse).astype(low).astype(wide)
    delta = jnp.sum(out * g.astype(wide).T, axis=0, keepdims=True)

    grad_query = jnp.zeros((HEAD_DIM, rows), wide)
    for kv, grad, base in ((near, near_grad, 0), (far, far_grad, half)):

        def back(i, grad_query, kv=kv, grad=grad, base=base):
            at = pl.multiple_of(i * step, step)
            p = score[pl.ds(base + at, step), :] * inverse
            gp = dot(kv[pl.ds(at, step), HEAD_DIM:], g, ((1,), (1,)))
            gs = (p * (gp - delta)).astype(low)
            grad[pl.ds(at, step), :HEAD_DIM] = (dot(gs, q, ((1,), (0,))) * scale).astype(low)
            grad[pl.ds(at, step), HEAD_DIM:] = dot(p.astype(low), g, ((1,), (0,))).astype(low)
            return grad_query + dot(kv[pl.ds(at, step), :HEAD_DIM], gs, ((0,), (0,)))

        grad_query = lax.fori_loop(0, half // step, back, grad_query, unroll=True)

    for i in range(heads):
        at, cols = slice(i * tok, (i + 1) * tok), slice(i * HEAD_DIM, (i + 1) * HEAD_DIM)
        att_gq[:, cols] = out[:, at].T.astype(low)
        back_cols = slice(heads * HEAD_DIM + cols.start, heads * HEAD_DIM + cols.stop)
        att_gq[:, back_cols] = turn(
            grad_query[:, at].T * scale, cosine[...], -sine[...]
        ).astype(low)


def attend(at_chx, query, grad_heads, near, far, bounds, cosine, sine):
    rows, tok = query.shape[0], cosine.shape[0]
    half = near.shape[0]
    vmem = pl.BlockSpec(memory_space=pltpu.VMEM)
    return pl.pallas_call(
        attend_kernel,
        in_specs=[pl.BlockSpec(memory_space=pltpu.SMEM)] + [vmem] * 7,
        out_shape=[
            jax.ShapeDtypeStruct((tok, 2 * rows // tok * HEAD_DIM), low),
            jax.ShapeDtypeStruct(near.shape, low),
            jax.ShapeDtypeStruct(far.shape, low),
        ],
        scratch_shapes=[pltpu.VMEM((2 * half, rows), wide)],
        compiler_params=PARAMS,
    )(at_chx, query, grad_heads, near, far, bounds, cosine, sine)


def back_project_kernel(att_gq, weights, waited, terms, grad):
    half = att_gq.shape[1] // 2
    terms[...] = dot(att_gq[:, :half], weights[:, half:], ((1,), (1,))).astype(low)
    grad[...] = dot(att_gq[:, half:], weights[:, :half], ((1,), (1,))).astype(low)


def back_project(att_gq, weights, waited, step=1024):
    tok = att_gq.shape[0]
    width, cols = weights.shape[0], att_gq.shape[1]
    out = pl.BlockSpec((tok, step), lambda i: (0, i))
    return pl.pallas_call(
        back_project_kernel,
        grid=(width // step,),
        in_specs=[
            pl.BlockSpec(att_gq.shape, lambda i: (0, 0)),
            pl.BlockSpec((step, cols), lambda i: (i, 0)),
            ANY,
        ],
        out_specs=[out, out],
        out_shape=[
            jax.ShapeDtypeStruct((tok, width), low),
            jax.ShapeDtypeStruct((tok, width), low),
        ],
        compiler_params=PARAMS,
    )(att_gq, weights, waited)


def normed_grad_kernel(query_terms, grad_kv, weights, normed, terms, gain):
    total = query_terms[...].astype(wide) + dot(grad_kv[...], weights[...], ((1,), (1,)))
    terms[...] = total.astype(low)
    gain[...] = jnp.sum(total * normed[...].astype(wide), axis=0, keepdims=True)


def normed_grad(query_terms, grad_kv, weights, both, step=1024):
    tok, width = query_terms.shape
    kv_cols = grad_kv.shape[1]
    at = weights.shape[1] // kv_cols - 1
    columns = pl.BlockSpec((tok, step), lambda i: (0, i))
    return pl.pallas_call(
        normed_grad_kernel,
        grid=(width // step,),
        in_specs=[
            columns,
            pl.BlockSpec((tok, kv_cols), lambda i: (0, 0)),
            pl.BlockSpec((step, kv_cols), lambda i: (i, at)),
            columns,
        ],
        out_specs=[columns, pl.BlockSpec((1, step), lambda i: (0, i))],
        out_shape=[
            jax.ShapeDtypeStruct((tok, width), low),
            jax.ShapeDtypeStruct((1, width), wide),
        ],
        compiler_params=PARAMS,
    )(query_terms, grad_kv, weights, both)


def positions(rows, at):
    return jnp.concatenate([part[j, at] for part in rows for j in range(2)], axis=0)


def weight_grad_kernel(*refs):
    rows, att_gq, grad_o, grad_q = refs[:NX], refs[NX], refs[-2], refs[-1]
    half, block = att_gq.shape[1] // 2, rows[0].shape[3] // 2

    @pl.when(pl.program_id(0) == 0)
    def _():
        grad_o[...] = jnp.zeros_like(grad_o)
        grad_q[...] = jnp.zeros_like(grad_q)

    own = jnp.concatenate([positions(rows, i) for i in range(rows[0].shape[1])], axis=0)
    grad_o[...] += dot(own[:, :block], att_gq[:, :half], ((0,), (0,)))
    grad_q[...] += dot(own[:, block:], att_gq[:, half:], ((0,), (0,)))


def weight_grads(rows, att_gq, step=8):
    two, n_dp, rows_own, both = rows[0].shape
    seq_len, cols = att_gq.shape
    out = jax.ShapeDtypeStruct((both // 2, cols // 2), wide)
    part = pl.BlockSpec((two, step, rows_own, both), lambda i: (0, i, 0, 0))
    return pl.pallas_call(
        weight_grad_kernel,
        grid=(n_dp // step,),
        in_specs=[part] * NX
        + [pl.BlockSpec((seq_len // n_dp * step, cols), lambda i: (i, 0))],
        out_specs=[pl.BlockSpec(out.shape, lambda i: (0, 0))] * 2,
        out_shape=[out, out],
        compiler_params=PARAMS,
    )(*rows, att_gq)


def kv_weight_grad_kernel(core, *refs):
    rows, (near, far, _, out, total, gains) = refs[:NX], refs[NX:]
    block = rows[0].shape[3] // 2
    tok = near.shape[1] - gains.shape[1]
    step = pl.program_id(0)

    @pl.when(step == 0)
    def _():
        total[...] = jnp.zeros_like(total)
        gains[...] = jnp.zeros_like(gains)

    c = core[0]
    own, grads = [], []
    for at, (grad, of) in enumerate(((near, c), (far, 1 - c))):
        for i in range(near.shape[0]):
            own.append(positions(rows, 2 * i + of)[:, block:])
            grads.append(grad[i, :tok])
            gains[at] += grad[i, tok:].astype(wide)
    own, grads = jnp.concatenate(own, axis=0), jnp.concatenate(grads, axis=0)
    total[...] += dot(own, grads, ((0,), (0,)))

    @pl.when(step == pl.num_programs(0) - 1)
    def _():
        out[: total.shape[0]] = total[...].astype(low)
        out[total.shape[0] :] = (gains[0] + gains[1]).astype(low)


def kv_weight_grad(core, rows, near, far, waited, tok, step=4):
    two, n_dp, rows_own, both = rows[0].shape
    outer, depth, cols = near.shape
    kv = pl.BlockSpec((step, depth, cols), lambda i, c: (i, 0, 0))
    part = pl.BlockSpec((two, 2 * step, rows_own, both), lambda i, c: (0, i, 0, 0))
    out = jax.ShapeDtypeStruct((both // 2 + depth - tok, cols), low)
    return pl.pallas_call(
        kv_weight_grad_kernel,
        grid_spec=pltpu.PrefetchScalarGridSpec(
            num_scalar_prefetch=1,
            grid=(outer // step,),
            in_specs=[part] * NX + [kv, kv, ANY],
            out_specs=pl.BlockSpec(out.shape, lambda i, c: (0, 0)),
            scratch_shapes=[
                pltpu.VMEM((both // 2, cols), wide),
                pltpu.VMEM((2, depth - tok, cols), wide),
            ],
        ),
        out_shape=out,
        compiler_params=PARAMS,
    )(core, *rows, near, far, waited)


def wait_kernel(value, waited, out):
    out[...] = value[...]


def wait(value, waited):
    return pl.pallas_call(
        wait_kernel,
        in_specs=[pl.BlockSpec(memory_space=pltpu.VMEM), ANY],
        out_shape=jax.ShapeDtypeStruct(value.shape, value.dtype),
        compiler_params=PARAMS,
    )(value, waited)


def pair_kernel(sums, waited, out):
    for i in range(2):
        out[i] = (sums[2 * i].astype(wide) + sums[2 * i + 1].astype(wide)).astype(low)


def pairs(sums, waited):
    return pl.pallas_call(
        pair_kernel,
        in_specs=[pl.BlockSpec(memory_space=pltpu.VMEM), ANY],
        out_shape=jax.ShapeDtypeStruct((NX // 2,) + sums.shape[1:], low),
        compiler_params=PARAMS,
    )(sums, waited)


def on_device(
    stream_in, pending, gain, q_weight, k_weight, v_weight, out_weight, grad_out, doc_ids
):
    y, z, c, h, x = (lax.axis_index(a) for a in ("y", "z", "c", "h", "x"))
    tens_index = h * NX + x
    rows_own, width = stream_in.shape
    tok = pending.shape[1]
    outer = SIZES["y"] * SIZES["z"]
    n_dp = outer * 2
    block = width // n_dp
    q_width = q_weight.shape[1]
    seq_len = doc_ids.shape[0]

    kv_first = tens_index * (q_width // HEAD_DIM) // (HEADS // KV_HEADS) * HEAD_DIM
    kv_weights = [
        lax.dynamic_slice_in_dim(w, kv_first, HEAD_DIM, 1) for w in (k_weight, v_weight)
    ]
    weights = lax.all_gather(
        jnp.concatenate([q_weight, out_weight], axis=1), DP, axis=0, tiled=True
    )
    near = spread(jnp.concatenate(kv_weights, axis=1), "z").reshape(-1, 2 * HEAD_DIM)
    near = spread(near, "y").reshape(outer, 1, block, 2 * HEAD_DIM)
    far = swap(near, "c")
    natural = [jnp.where(c == 0, near, far), jnp.where(c == 0, far, near)]
    wkv = jnp.concatenate(natural, axis=1).reshape(width, 2 * HEAD_DIM)

    stream_f = stream_in.astype(wide)
    inv_rms = lax.rsqrt(jnp.mean(stream_f * stream_f, axis=-1, keepdims=True) + eps)
    unit_rows = stream_f * inv_rms
    normed_own = (unit_rows * gain).astype(low)
    both = spread_h(jnp.concatenate([normed_own, grad_out], axis=1))
    both = jnp.stack(spread_x(both)).reshape(tok, 2 * width)

    split = [a.reshape(rows_own, n_dp, block) for a in (grad_out, normed_own)]
    rows = jnp.transpose(jnp.concatenate(split, axis=2), (1, 0, 2))

    def index(axis):
        return lax.broadcasted_iota(jnp.int32, (NX, 2, rows_own), axis)

    local = (((h ^ index(1)) * NX + (x + index(0)) % NX) * rows_own + index(2)).reshape(tok)
    block_first = ((y * SIZES["z"] + z) * 2 + c) * tok
    places = block_first + local
    def relative(a):
        a = a.reshape((2, NX, rows_own) + a.shape[1:])
        a = jnp.where(h == 0, a, a[::-1])
        a = lax.dynamic_slice_in_dim(jnp.concatenate([a, a], axis=1), x, NX, 1)
        return jnp.swapaxes(a, 0, 1)

    doc_query = relative(lax.dynamic_slice_in_dim(doc_ids, block_first, tok)).reshape(tok)
    first_place = jnp.sum((doc_ids[None, :] < doc_query[:, None]).astype(jnp.int32), axis=1)

    frequency = rope_base ** (-2.0 * jnp.arange(HALF_DIM).astype(wide) / HEAD_DIM)
    angles = places.astype(wide)[:, None] * frequency[None, :]
    cosine, sine = jnp.cos(angles), jnp.sin(angles)
    cosine = jnp.concatenate([cosine, cosine], axis=1)
    sine = jnp.concatenate([-sine, sine], axis=1)

    def rotate(field, sign):
        flipped = jnp.concatenate([field[:, HALF_DIM:], field[:, :HALF_DIM]], axis=1)
        return field * cosine + sign * flipped * sine

    pend = relative(pending[0])
    bounds = jnp.stack([places, first_place])
    both, pend, bounds, cosine, sine = lax.optimization_barrier(
        (both, pend, bounds, cosine, sine)
    )
    kv_own = kv_project(both, wkv, cosine, sine)
    kv_near = spread(kv_own, "z").reshape(-1, 2 * HEAD_DIM)
    query, grad_heads = project(both, weights, cosine, sine, 2 * q_width)
    kv_near = spread(kv_near, "y").reshape(-1, 2 * HEAD_DIM)
    kv_far = swap(kv_near, "c")
    rows = lax.all_to_all(wait(rows, kv_near), DP, 0, 0, tiled=True)
    at_chx = jnp.stack([c, h, x]).astype(jnp.int32)
    att_gq, near_piece, far_piece = attend(
        at_chx, query, grad_heads, kv_near, kv_far, bounds, cosine, sine
    )
    att_gq_all = lax.all_gather(wait(att_gq, rows), DP, axis=0, tiled=True)
    kv_sum = near_piece.astype(wide) + swap(far_piece, "c").astype(wide)
    kv_sum = kv_sum.astype(low).reshape(SIZES["y"], -1, 2 * HEAD_DIM)
    rows = wait(rows, kv_sum)
    rows = spread_h(rows)
    terms, query_terms = back_project(att_gq, weights, rows)
    kv_sum = collect(kv_sum, "y").astype(low)
    kv_grad = collect(kv_sum.reshape(SIZES["z"], tok, 2 * HEAD_DIM), "z")
    grad_key = rotate(kv_grad[:, :HEAD_DIM], -1.0)
    grad_kv = jnp.concatenate([grad_key, kv_grad[:, HEAD_DIM:]], axis=1).astype(low)

    terms = terms.reshape(NX, 2, rows_own, width).astype(wide) + pend.astype(wide)
    hidden_part, hidden_other = collect_x(terms.astype(low))

    normed_terms, gain_terms = normed_grad(query_terms, grad_kv, wkv, both)
    gain_rows = gain_terms.astype(low).reshape(-1, 2 * HEAD_DIM)
    depth = tok + gain_rows.shape[0]
    near = spread(jnp.concatenate([grad_kv, gain_rows], axis=0), "z")
    near = spread(near, "y").reshape(outer, depth, 2 * HEAD_DIM)
    rows = spread_x(rows)
    hidden_other = swap(hidden_other, "h")
    sums = kv_weight_grad(
        c.astype(jnp.int32)[None], rows, near, swap(near, "c"), hidden_other, tok
    )

    normed_part, normed_other = collect_x(normed_terms.reshape(NX, 2, rows_own, width))
    normed_other = swap(wait(normed_other, sums), "h")
    grad_normed = normed_part + normed_other.astype(wide)
    hidden_out = (stream_f + (hidden_part + hidden_other.astype(wide))).astype(low)

    sums = spread(sums, "x")
    grad_o, grad_q = weight_grads(rows, att_gq_all)
    sums = pairs(sums, grad_o)
    sums_other = swap(sums, "h")
    pair, other = sums[:, :block], sums_other[:, :block]
    gain_sum = sum_pair(sums[:, block:]) + sum_pair(sums_other[:, block:])
    grad_gain = gain_sum.reshape(width) / gain
    first, second = jnp.where(h == 0, pair, other), jnp.where(h == 0, other, pair)
    heads = [first[0], first[1], second[0], second[1]]
    grad_k, grad_v = (
        jnp.concatenate([a[:, i : i + HEAD_DIM] for a in heads], axis=1).astype(wide)
        for i in (0, HEAD_DIM)
    )

    scaled_grad = grad_normed * gain
    grad_stream = (
        inv_rms
        * (scaled_grad - unit_rows * jnp.mean(scaled_grad * unit_rows, axis=-1, keepdims=True))
        + grad_out.astype(wide)
    ).astype(low)
    return (hidden_out, grad_stream, grad_gain, grad_q, grad_k, grad_v, grad_o)


def solution(mesh):
    fine = Mesh(mesh.devices.reshape(tuple(SIZES.values())), tuple(SIZES))
    whole = P(DP + TENSOR, None)
    in_specs = (
        whole,
        P(TENSOR, DP, None),
        P(),
        P(DP, TENSOR),
        P(DP, None),
        P(DP, None),
        P(DP, TENSOR),
        whole,
        P(),
    )
    out_specs = (whole, whole, P(), P(DP, TENSOR), P(DP, None), P(DP, None), P(DP, TENSOR))
    return jax.shard_map(
        on_device, mesh=fine, in_specs=in_specs, out_specs=out_specs, check_vma=False
    )
```
